256 devices in a mesh: dp: 16 (over z, core), mp: 16 (over x, y).
Axes of the slice: x: 4, y: 4, z: 8, core: 2. Of those that a mesh axis runs over, the one named last changes fastest.
Arguments:
- queries: bfloat16 [8192, 4096], P('dp', 'mp'), may hold values from -60 to 60
- grad_attn: bfloat16 [8192, 4096], P('dp', 'mp'), may hold values from -6 to 6
- encoded: bfloat16 [8192, 4096], P('dp', 'mp'), may hold values from -6 to 6
- key_weight: bfloat16 [4096, 4096], P(None, 'mp'), may hold values from -0.09375 to 0.09375
- value_weight: bfloat16 [4096, 4096], P(None, 'mp'), may hold values from -0.09375 to 0.09375
- nbr_ids: int32 [128, 2], P('dp'), may hold values from 0 to 63, as said below
Outputs:
- query_grad: bfloat16 [8192, 4096], P('dp', 'mp')
- encoded_grad: bfloat16 [8192, 4096], P('dp', 'mp')
- key_weight_grad: float32 [4096, 4096], P('dp', 'mp')
- value_weight_grad: float32 [4096, 4096], P('dp', 'mp')
The draws below stay inside these ranges and needn't reach their ends.
Inputs may be any that keep to these rules, and one draw needn't show every extreme that they name: `nbr_ids`: of the 16 slots of one index of dp, at most 2 name blocks of one owner (owner = id // 4); in every draw one owner gets exactly 2 from every index. The 2 neighbours of a span differ.
All inputs are finite; a program needn't handle non-finite values.
Results may differ from the reference program's by a relative error of at most 0.015.
The reference program's roundings to bfloat16 on the way (of `prob_rounded` and `score_grad`) count: a program that leaves them out, or rounds other values in their place, can miss the bound.
Values may be sent and summed in bfloat16 or wider, within the bound.
A program may use at most 128 MiB of HBM per device.

```python
import math
import jax
import jax.numpy as jnp
from jax import lax

D = 4096
H = 32
HD = 128
SPAN = 64
NL = 128
K = 2
CH_DEV = 8
NB_DEV = 4
CAP = 2
TOKENS = 8192
SPANS = 128
NBR = 64
N_DP = 16


def draw_queries(key, part):
    key = jax.random.fold_in(key, 5)
    return jnp.clip(jax.random.normal(key, (TOKENS, D), jnp.float32), -6.0, 6.0).astype(jnp.bfloat16)


def draw_nbr_ids(key, part):
    key = jax.random.fold_in(key, 11)
    slot_count = CH_DEV * K
    hot_owner = jax.random.randint(jax.random.fold_in(key, 1), (), 0, N_DP)
    owner_pool = jnp.arange(N_DP * CAP, dtype=jnp.int32) // CAP
    within_owner = jnp.arange(N_DP * CAP, dtype=jnp.int32) % CAP

    def draw_device(device_key):
        key_pick, key_group, key_offset = jax.random.split(device_key, 3)
        shuffled = jax.random.permutation(key_pick, N_DP * CAP).astype(jnp.int32)
        priority = jnp.where(owner_pool == hot_owner, within_owner, CAP + shuffled)
        chosen = owner_pool[jnp.argsort(priority)[:slot_count]]
        owner_order = jax.random.permutation(key_group, N_DP).astype(jnp.int32)
        regroup = jnp.argsort(owner_order[chosen] * slot_count + jnp.arange(slot_count, dtype=jnp.int32))
        owners = chosen[regroup]
        position = jnp.arange(slot_count, dtype=jnp.int32)
        alike = (owners[:, None] == owners[None, :]) & (position[None, :] < position[:, None])
        rank_within = jnp.sum(alike.astype(jnp.int32), axis=1)
        offset = jax.random.randint(key_offset, (N_DP,), 0, NB_DEV).astype(jnp.int32)
        return owners * NB_DEV + (rank_within + offset[owners]) % NB_DEV
    device_keys = jax.random.split(jax.random.fold_in(key, 2), N_DP)
    return jax.vmap(draw_device)(device_keys).reshape(N_DP * CH_DEV, K).astype(jnp.int32)


def shard_levels(rng, shape, cuts, low, high):
    loudness, own = 1.0, jax.random.fold_in(rng, 6)
    for axis_at, blocks in cuts:
        draws = jnp.exp(jax.random.uniform(jax.random.fold_in(own, axis_at), (blocks,), jnp.float32, low / len(cuts), high / len(cuts)))
        loudness = loudness * jnp.repeat(draws, shape[axis_at] // blocks).reshape([-1 if axis == axis_at else 1 for axis in range(len(shape))])
    return loudness


def scatter_about(stream_key, shape, deviation, most, cuts=(), kind=jnp.bfloat16):
    values = deviation * jax.random.normal(stream_key, shape, jnp.float32)
    if cuts:
        values = values * shard_levels(stream_key, shape, cuts, -0.22, 0.18)
    return jnp.clip(values, -most, most).astype(kind)


def setup_inputs(seed: int = 0) -> dict:
    key_list = jax.random.split(jax.random.key(seed), 7)
    return {
        "queries": draw_queries(jax.random.fold_in(key_list[6], 71), 0),
        "grad_attn": scatter_about(key_list[1], (TOKENS, D), 1.0, 6.0, ((0, 16), (1, 16))),
        "encoded": scatter_about(key_list[2], (NBR * NL, D), 1.0, 6.0, ((0, 16), (1, 16))),
        "key_weight": scatter_about(key_list[3], (D, D), D ** -0.5, 0.09375, ((1, 16),)),
        "value_weight": scatter_about(key_list[4], (D, D), D ** -0.5, 0.09375, ((1, 16),)),
        "nbr_ids": draw_nbr_ids(jax.random.fold_in(key_list[6], 71), 0),
    }


def reference(queries, grad_attn, encoded, key_weight, value_weight, nbr_ids):
    scale = 1.0 / math.sqrt(HD)
    key_table = jnp.dot(encoded, key_weight, preferred_element_type=jnp.float32).astype(jnp.bfloat16).reshape(NBR, NL, D)
    value_table = jnp.dot(encoded, value_weight, preferred_element_type=jnp.float32).astype(jnp.bfloat16).reshape(NBR, NL, D)
    query_all = queries.reshape(SPANS, SPAN, H, HD)
    grad_all = grad_attn.reshape(SPANS, SPAN, H, HD)

    def one_span(inputs):
        query_rows, grad_rows, span_ids = inputs
        key_rows = key_table[span_ids].reshape(K * NL, H, HD).astype(jnp.float32)
        value_rows = value_table[span_ids].reshape(K * NL, H, HD).astype(jnp.float32)
        query_float = query_rows.astype(jnp.float32)
        grad_float = grad_rows.astype(jnp.float32)
        scores = jnp.einsum('qhd,khd->hqk', query_float, key_rows) * scale
        attn_prob = jax.nn.softmax(scores, axis=-1)
        prob_rounded = lax.optimization_barrier(attn_prob.astype(jnp.bfloat16)).astype(jnp.float32)
        prob_grad = jnp.einsum('qhd,khd->hqk', grad_float, value_rows)
        delta = lax.optimization_barrier(jnp.sum(attn_prob * prob_grad, axis=-1, keepdims=True))
        score_grad = (attn_prob * (prob_grad - delta) * scale).astype(jnp.bfloat16)
        score_grad = lax.optimization_barrier(score_grad).astype(jnp.float32)
        query_grad = jnp.einsum('hqk,khd->qhd', score_grad, key_rows).astype(jnp.bfloat16).reshape(SPAN, D)
        slot_key = jnp.einsum('hqk,qhd->khd', score_grad, query_float).astype(jnp.bfloat16).reshape(K, NL, D)
        slot_value = jnp.einsum('hqk,qhd->khd', prob_rounded, grad_float).astype(jnp.bfloat16).reshape(K, NL, D)
        return (query_grad, slot_key, slot_value)
    query_grad, slot_key, slot_value = lax.map(one_span, (query_all, grad_all, nbr_ids))
    flat_ids = nbr_ids.reshape(SPANS * K).astype(jnp.int32)
    block_key = jnp.zeros((NBR, NL, D), jnp.float32).at[flat_ids].add(slot_key.reshape(SPANS * K, NL, D).astype(jnp.float32))
    block_value = jnp.zeros((NBR, NL, D), jnp.float32).at[flat_ids].add(slot_value.reshape(SPANS * K, NL, D).astype(jnp.float32))
    block_key = block_key.astype(jnp.bfloat16).reshape(NBR * NL, D)
    block_value = block_value.astype(jnp.bfloat16).reshape(NBR * NL, D)
    contract_cols = (((1,), (1,)), ((), ()))
    encoded_grad = lax.dot_general(block_key, key_weight, contract_cols, preferred_element_type=jnp.float32)
    encoded_grad = encoded_grad + lax.dot_general(block_value, value_weight, contract_cols, preferred_element_type=jnp.float32)
    contract_rows = (((0,), (0,)), ((), ()))
    key_weight_grad = lax.dot_general(encoded, block_key, contract_rows, preferred_element_type=jnp.float32)
    value_weight_grad = lax.dot_general(encoded, block_value, contract_rows, preferred_element_type=jnp.float32)
    return (query_grad.reshape(TOKENS, D), encoded_grad.astype(jnp.bfloat16), key_weight_grad, value_weight_grad)
```

```python
import math

import jax
import jax.numpy as jnp
from jax import lax
from jax.experimental import pallas as pl
from jax.experimental.pallas import tpu as pltpu
from jax.sharding import PartitionSpec as P

HD = 128
SPAN = 64
NL = 128
K = 2
NB_DEV = 4
DP = 16
MP = 16
ZN = 8
SIDE = 4
SHARD = 256
ROWS = 512
HALF = 256
CHUNK = 128
SLOTS = 32
MESH = pl.DeviceIdType.MESH
SCALE = 1.0 / math.sqrt(HD)
OFFSETS = (0, -1, 1, 2)
NT = (((1,), (1,)), ((), ()))
NN = (((1,), (0,)), ((), ()))
TN = (((0,), (0,)), ((), ()))


def dot(a, b, dims):
    return lax.dot_general(a, b, dims, preferred_element_type=jnp.float32)


def wrap(value, size):
    return lax.rem(value + size, size)


class Place:
    def __init__(self):
        self.dp = lax.axis_index("dp")
        self.mp = lax.axis_index("mp")
        self.z, self.core = lax.div(self.dp, 2), lax.rem(self.dp, 2)
        self.x, self.y = lax.div(self.mp, SIDE), lax.rem(self.mp, SIDE)
        self.sibling = self.z * 2 + 1 - self.core

    def along_z(self, step, other_core=False):
        core = 1 - self.core if other_core else self.core
        return wrap(self.z + step, ZN) * 2 + core

    def in_plane(self, path, first, second):
        along_x, along_y = (first, second) if path == 0 else (second, first)
        return wrap(self.x + along_x, SIDE) * SIDE + wrap(self.y + along_y, SIDE)

    def plane_neighbour(self, path, axis, way):
        step = 1 if way == 0 else -1
        return self.in_plane(path, step, 0) if axis == 0 else self.in_plane(path, 0, step)

    def z_device(self, way):
        return (self.along_z(1 if way == 0 else -1), self.mp)

    def greet(self, plane=True):
        others = [self.z_device(0), self.z_device(1), (self.sibling, self.mp)]
        if plane:
            others += [(self.dp, self.plane_neighbour(0, axis, way)) for axis in (0, 1) for way in (0, 1)]
        barrier = pltpu.get_barrier_semaphore()
        for device in others:
            pl.semaphore_signal(barrier, inc=1, device_id=device, device_id_type=MESH)
        pl.semaphore_wait(barrier, len(others))


class Sends:
    def __init__(self):
        self.started = []

    def send(self, src, dst, send_sem, recv_sem, device):
        copy = pltpu.make_async_remote_copy(
            src_ref=src,
            dst_ref=dst,
            send_sem=send_sem,
            recv_sem=recv_sem,
            device_id=device,
            device_id_type=MESH,
        )
        copy.start()
        self.started.append(copy)

    def finish(self):
        for copy in self.started:
            copy.wait_send()


def landed(ref, sem):
    pltpu.make_async_copy(ref, ref, sem).wait()


def gather_kernel(
    q_ref, g_ref, e_ref, ids_ref, kw_ref, vw_ref,
    q_all, g_all, enc_out, kv_ref, ids_all,
    enc, kw, vw, acc, local_sem, zs, zr, cs, cr, p1s, p1r, p2s, p2r,
):
    at = Place()
    out = Sends()
    srcs, alls = (q_ref, g_ref, ids_ref), (q_all, g_all, ids_all)
    at.greet()

    def z_send(way, step, kind):
        origin = at.along_z(1 - step if way == 0 else step - 1)
        src = srcs[kind] if step == 1 else alls[kind].at[origin]
        out.send(src, alls[kind].at[origin], zs.at[way, step - 1, kind], zr.at[way, step - 1, kind], at.z_device(way))

    def core_send(which, kind, origin, src):
        out.send(src, alls[kind].at[origin], cs.at[which, kind], cr.at[which, kind], (at.sibling, at.mp))

    def carries(way, step, kind):
        return step < 4 or (step == 4 and (way == 1) == (kind == 1))

    def z_arrive(way, step, kind):
        origin = at.along_z(-step if way == 0 else step)
        landed(alls[kind].at[origin], zr.at[way, step - 1, kind])
        if carries(way, step + 1, kind):
            z_send(way, step + 1, kind)
        core_send(way * 4 + step, kind, origin, alls[kind].at[origin])

    def rows_of(path):
        return pl.ds(path * HALF, HALF)

    def part_of(path, way):
        return pl.ds(path * HALF + way * CHUNK, CHUNK)

    def p2_first(path, k):
        origin = at.in_plane(path, OFFSETS[k], 0)
        dst = enc.at[origin, rows_of(path)]
        src = e_ref.at[rows_of(path)] if k == 0 else dst
        for way in (0, 1):
            device = (at.dp, at.plane_neighbour(path, 1, way))
            out.send(src, dst, p2s.at[path, k, way], p2r.at[path, k, way], device)

    def p1_first(path):
        for way in (0, 1):
            device = (at.dp, at.plane_neighbour(path, 0, way))
            out.send(
                e_ref.at[rows_of(path)], enc.at[at.mp, rows_of(path)],
                p1s.at[path, way], p1r.at[path, way], device,
            )

    def p1_arrive(path, way):
        origin = at.in_plane(path, -1 if way == 0 else 1, 0)
        landed(enc.at[origin, rows_of(path)], p1r.at[path, way])
        part = enc.at[origin, part_of(path, way)]
        device = (at.dp, at.plane_neighbour(path, 0, way))
        out.send(part, part, p1s.at[path, 2 + way], p1r.at[path, 2 + way], device)
        p2_first(path, 1 + way)

    def p1_far(path):
        origin = at.in_plane(path, 2, 0)
        for way in (0, 1):
            landed(enc.at[origin, part_of(path, way)], p1r.at[path, 2 + way])
        p2_first(path, 3)

    def p2_arrive(path, k):
        for way in (0, 1):
            origin = at.in_plane(path, OFFSETS[k], -1 if way == 0 else 1)
            landed(enc.at[origin, rows_of(path)], p2r.at[path, k, way])
            part = enc.at[origin, part_of(path, way)]
            device = (at.dp, at.plane_neighbour(path, 1, way))
            out.send(part, part, p2s.at[path, k, 2 + way], p2r.at[path, k, 2 + way], device)

    def p2_far(path, k):
        origin = at.in_plane(path, OFFSETS[k], 2)
        for way in (0, 1):
            landed(enc.at[origin, part_of(path, way)], p2r.at[path, k, 2 + way])

    def project(batch):
        def one(j, carry):
            rows = pl.ds(pl.multiple_of(j * SHARD, SHARD), SHARD)
            block = enc[j]
            acc[:, :SHARD] += dot(block, kw[rows, :], NN)
            acc[:, SHARD:] += dot(block, vw[rows, :], NN)
            return carry

        lax.fori_loop(batch * 4, batch * 4 + 4, one, 0)

    for way in (0, 1):
        z_send(way, 1, 2)
    for kind in (0, 1):
        for way in (0, 1):
            z_send(way, 1, kind)
    for path in (0, 1):
        p1_first(path)
    for path in (0, 1):
        p2_first(path, 0)
    for kind in (2, 0, 1):
        core_send(0, kind, at.dp, srcs[kind])
    locals_ = [
        pltpu.make_async_copy(e_ref, enc.at[at.mp], local_sem.at[0]),
        pltpu.make_async_copy(kw_ref, kw, local_sem.at[1]),
        pltpu.make_async_copy(vw_ref, vw, local_sem.at[2]),
        pltpu.make_async_copy(q_ref, q_all.at[at.dp], local_sem.at[3]),
        pltpu.make_async_copy(g_ref, g_all.at[at.dp], local_sem.at[4]),
        pltpu.make_async_copy(ids_ref, ids_all.at[at.dp], local_sem.at[5]),
    ]
    for copy in locals_:
        copy.start()
    acc[...] = jnp.zeros_like(acc)

    for way in (0, 1):
        for path in (0, 1):
            p1_arrive(path, way)
    for way in (0, 1):
        z_arrive(way, 1, 2)
    for path in (0, 1):
        p2_arrive(path, 0)
    for way in (0, 1):
        z_arrive(way, 1, 0)
    for path in (0, 1):
        p1_far(path)
    for way in (0, 1):
        z_arrive(way, 2, 2)
    for path in (0, 1):
        p2_arrive(path, 1)
    for way in (0, 1):
        z_arrive(way, 1, 1)
    for path in (0, 1):
        p2_arrive(path, 2)
    for way in (0, 1):
        z_arrive(way, 3, 2)
    for way in (0, 1):
        z_arrive(way, 2, 0)
    for path in (0, 1):
        p2_arrive(path, 3)
    for k in range(4):
        for path in (0, 1):
            p2_far(path, k)
    for copy in locals_:
        copy.wait()
    write_enc = pltpu.make_async_copy(enc, enc_out, local_sem.at[0])
    write_enc.start()
    for way in (0, 1):
        z_arrive(way, 2, 1)
    project(0)
    z_arrive(0, 4, 2)
    for way in (0, 1):
        z_arrive(way, 3, 0)
    project(1)
    for way in (0, 1):
        z_arrive(way, 3, 1)
    project(2)
    project(3)
    kv_ref[...] = acc[...].astype(jnp.bfloat16)
    z_arrive(0, 4, 0)
    z_arrive(1, 4, 1)
    for kind in (0, 1, 2):
        landed(alls[kind].at[at.sibling], cr.at[0, kind])
        for way in (0, 1):
            for step in range(1, 5):
                if carries(way, step, kind):
                    origin = at.along_z(-step if way == 0 else step, other_core=True)
                    landed(alls[kind].at[origin], cr.at[way * 4 + step, kind])
    write_enc.wait()
    out.finish()


def gather(queries, grad_attn, encoded, ids, key_weight, value_weight):
    any_ = pl.BlockSpec(memory_space=pl.ANY)
    vmem = pl.BlockSpec(memory_space=pltpu.VMEM)
    dma = pltpu.SemaphoreType.DMA
    bf16 = jnp.bfloat16
    return pl.pallas_call(
        gather_kernel,
        out_shape=(
            jax.ShapeDtypeStruct((DP, ROWS, SHARD), bf16),
            jax.ShapeDtypeStruct((DP, ROWS, SHARD), bf16),
            jax.ShapeDtypeStruct((MP, ROWS, SHARD), bf16),
            jax.ShapeDtypeStruct((ROWS, 2 * SHARD), bf16),
            jax.ShapeDtypeStruct((DP, 8, 128), jnp.int32),
        ),
        in_specs=[any_, any_, any_, vmem, any_, any_],
        out_specs=(any_, any_, any_, vmem, vmem),
        scratch_shapes=[
            pltpu.VMEM((MP, ROWS, SHARD), bf16),
            pltpu.VMEM((MP * SHARD, SHARD), bf16),
            pltpu.VMEM((MP * SHARD, SHARD), bf16),
            pltpu.VMEM((ROWS, 2 * SHARD), jnp.float32),
            dma((6,)),
            dma((2, 4, 3)), dma((2, 4, 3)),
            dma((9, 3)), dma((9, 3)),
            dma((2, 4)), dma((2, 4)),
            dma((2, 4, 4)), dma((2, 4, 4)),
        ],
        compiler_params=pltpu.CompilerParams(
            collective_id=0, has_side_effects=True, vmem_limit_bytes=40 * 2**20
        ),
        name="gather_all",
    )(queries, grad_attn, encoded, ids, key_weight, value_weight)


def fetch_slots(table, q_all, g_all, qs, gs, sem):
    def issue(p, carry):
        rows = pl.ds(pl.multiple_of(table[p] * SPAN, SPAN), SPAN)
        to = pl.ds(pl.multiple_of(p * SPAN, SPAN), SPAN)
        requester = lax.div(p, 2)
        pltpu.make_async_copy(q_all.at[requester, rows], qs.at[to], sem.at[0]).start()
        pltpu.make_async_copy(g_all.at[requester, rows], gs.at[to], sem.at[1]).start()
        return carry

    lax.fori_loop(0, SLOTS, issue, 0)
    landed(qs, sem.at[0])
    landed(gs, sem.at[1])


def block_rows(table, p):
    return pl.ds(pl.multiple_of(table[SLOTS + p] * NL, NL), NL)


def slot_products(kv, blocks, head, q_rows, g_rows, first):
    cols = slice(head * HD, (head + 1) * HD)
    vcols = slice(SHARD + head * HD, SHARD + (head + 1) * HD)
    qh, gh = q_rows[:, cols], g_rows[:, cols]
    keys = [kv[rows, cols] for rows in blocks]
    values = [kv[rows, vcols] for rows in blocks]
    scores = jnp.where(first, dot(keys[0], qh, NT), dot(keys[1], qh, NT)) * SCALE
    prob_grad = jnp.where(first, dot(values[0], gh, NT), dot(values[1], gh, NT))
    return qh, gh, keys, scores, prob_grad


def stats_kernel(table, q_all, g_all, kv, stats, qs, gs, sem):
    fetch_slots(table, q_all, g_all, qs, gs, sem)
    first = lax.broadcasted_iota(jnp.int32, (NL, 2 * SPAN), 1) < SPAN

    def one(i, carry):
        rows = pl.ds(pl.multiple_of(i * 2 * SPAN, 2 * SPAN), 2 * SPAN)
        q_rows, g_rows = qs[rows, :], gs[rows, :]
        blocks = [block_rows(table, 2 * i), block_rows(table, 2 * i + 1)]
        for head in (0, 1):
            _, _, _, scores, prob_grad = slot_products(kv, blocks, head, q_rows, g_rows, first)
            top = jnp.max(scores, axis=0, keepdims=True)
            e = jnp.exp(scores - top)
            total = jnp.sum(e, axis=0, keepdims=True)
            stats[pl.ds(i * 4 + head, 1), :] = top + jnp.log(total)
            stats[pl.ds(i * 4 + 2 + head, 1), :] = jnp.sum(e * prob_grad, axis=0, keepdims=True) / total
        return carry

    lax.fori_loop(0, DP, one, 0)


def slot_stats(table, q_all, g_all, kv):
    any_ = pl.BlockSpec(memory_space=pl.ANY)
    vmem = pl.BlockSpec(memory_space=pltpu.VMEM)
    return pl.pallas_call(
        stats_kernel,
        out_shape=jax.ShapeDtypeStruct((DP * 4, 128), jnp.float32),
        in_specs=[pl.BlockSpec(memory_space=pltpu.SMEM), any_, any_, vmem],
        out_specs=vmem,
        scratch_shapes=[
            pltpu.VMEM((SLOTS * SPAN, SHARD), jnp.bfloat16),
            pltpu.VMEM((SLOTS * SPAN, SHARD), jnp.bfloat16),
            pltpu.SemaphoreType.DMA((2,)),
        ],
        compiler_params=pltpu.CompilerParams(vmem_limit_bytes=40 * 2**20),
        name="slot_stats",
    )(table, q_all, g_all, kv)


def share_kernel(stats, all_stats, local_sem, zs, zr, cs, cr):
    at = Place()
    out = Sends()
    at.greet(plane=False)

    def z_send(way, step):
        origin = at.along_z(1 - step if way == 0 else step - 1)
        src = stats if step == 1 else all_stats.at[origin]
        out.send(src, all_stats.at[origin], zs.at[way, step - 1], zr.at[way, step - 1], at.z_device(way))

    def core_send(which, origin, src):
        out.send(src, all_stats.at[origin], cs.at[which], cr.at[which], (at.sibling, at.mp))

    for way in (0, 1):
        z_send(way, 1)
    core_send(0, at.dp, stats)
    own = pltpu.make_async_copy(stats, all_stats.at[at.dp], local_sem.at[0])
    own.start()
    for step in range(1, 5):
        for way in (0, 1):
            if step == 4 and way == 1:
                continue
            origin = at.along_z(-step if way == 0 else step)
            landed(all_stats.at[origin], zr.at[way, step - 1])
            if step < 3 or (step == 3 and way == 0):
                z_send(way, step + 1)
            core_send(way * 4 + step, origin, all_stats.at[origin])
    own.wait()
    landed(all_stats.at[at.sibling], cr.at[0])
    for step in range(1, 5):
        for way in (0, 1):
            if step == 4 and way == 1:
                continue
            origin = at.along_z(-step if way == 0 else step, other_core=True)
            landed(all_stats.at[origin], cr.at[way * 4 + step])
    out.finish()


def share_stats(stats):
    vmem = pl.BlockSpec(memory_space=pltpu.VMEM)
    dma = pltpu.SemaphoreType.DMA
    return pl.pallas_call(
        share_kernel,
        out_shape=jax.ShapeDtypeStruct((DP, DP * 4, 128), jnp.float32),
        in_specs=[vmem],
        out_specs=vmem,
        scratch_shapes=[dma((1,)), dma((2, 4)), dma((2, 4)), dma((9,)), dma((9,))],
        compiler_params=pltpu.CompilerParams(
            collective_id=1, has_side_effects=True, vmem_limit_bytes=40 * 2**20
        ),
        name="share_stats",
    )(stats)


def grads_kernel(table, q_all, g_all, kv, all_stats, block_grad, dq, qs, gs, acc, sem):
    def clear(i, carry):
        dq[i] = jnp.zeros((ROWS, SHARD), jnp.bfloat16)
        return carry

    fetch_slots(table, q_all, g_all, qs, gs, sem)
    lax.fori_loop(0, DP, clear, 0)
    acc[...] = jnp.zeros_like(acc)
    me = table[5 * SLOTS]
    lanes = lax.broadcasted_iota(jnp.int32, (NL, 2 * SPAN), 1)
    first = lanes < SPAN
    first_row = lax.broadcasted_iota(jnp.int32, (1, 2 * SPAN), 1) < SPAN

    def one(i, carry):
        rows = pl.ds(pl.multiple_of(i * 2 * SPAN, 2 * SPAN), 2 * SPAN)
        q_rows, g_rows = qs[rows, :], gs[rows, :]
        blocks = [block_rows(table, 2 * i), block_rows(table, 2 * i + 1)]
        filled = [table[4 * SLOTS + 2 * i + rank] for rank in (0, 1)]
        keep = jnp.where(first, filled[0], filled[1]) > 0

        def partner(stat):
            found = []
            for rank in (0, 1):
                owner = table[2 * SLOTS + 2 * i + rank]
                there = table[3 * SLOTS + 2 * i + rank]
                row = all_stats[owner, pl.ds(i * 4 + stat, 1), :]
                found.append(jnp.where(there == rank, row, pltpu.roll(row, SPAN, 1)))
            return jnp.where(first_row, found[0], found[1])

        for head in (0, 1):
            cols = slice(head * HD, (head + 1) * HD)
            vcols = slice(SHARD + head * HD, SHARD + (head + 1) * HD)
            qh, gh, keys, scores, prob_grad = slot_products(kv, blocks, head, q_rows, g_rows, first)
            lse_here = all_stats[me, pl.ds(i * 4 + head, 1), :]
            lse_there = partner(head)
            delta_here = all_stats[me, pl.ds(i * 4 + 2 + head, 1), :]
            delta_there = partner(2 + head)
            top = jnp.maximum(lse_here, lse_there)
            lse = top + jnp.log(jnp.exp(lse_here - top) + jnp.exp(lse_there - top))
            delta = jnp.exp(lse_here - lse) * delta_here + jnp.exp(lse_there - lse) * delta_there
            prob = jnp.exp(scores - lse)
            score_grad = prob * (prob_grad - delta) * SCALE
            zero = jnp.zeros_like(prob)
            prob = jnp.where(keep, prob, zero)
            score_grad = jnp.where(keep, score_grad, zero)
            parts = [(first, 0), (jnp.logical_not(first), 1)]
            for mask, rank in parts:
                ds = jnp.where(mask, score_grad, zero).astype(jnp.bfloat16)
                pr = jnp.where(mask, prob, zero).astype(jnp.bfloat16)
                acc[blocks[rank], cols] += dot(ds, qh, NN)
                acc[blocks[rank], vcols] += dot(pr, gh, NN)
                span = table[2 * i + rank]
                where = pl.ds(pl.multiple_of(span * SPAN, SPAN), SPAN)
                dq_rows = dot(ds, keys[rank], TN)[rank * SPAN : (rank + 1) * SPAN, :]
                old = dq[i, where, cols].astype(jnp.float32)
                dq[i, where, cols] = (old + dq_rows).astype(jnp.bfloat16)
        return carry

    lax.fori_loop(0, DP, one, 0)
    block_grad[...] = acc[...].astype(jnp.bfloat16)


def slot_grads(table, q_all, g_all, kv, all_stats):
    any_ = pl.BlockSpec(memory_space=pl.ANY)
    vmem = pl.BlockSpec(memory_space=pltpu.VMEM)
    return pl.pallas_call(
        grads_kernel,
        out_shape=(
            jax.ShapeDtypeStruct((ROWS, 2 * SHARD), jnp.bfloat16),
            jax.ShapeDtypeStruct((DP, ROWS, SHARD), jnp.bfloat16),
        ),
        in_specs=[pl.BlockSpec(memory_space=pltpu.SMEM), any_, any_, vmem, vmem],
        out_specs=(vmem, vmem),
        scratch_shapes=[
            pltpu.VMEM((SLOTS * SPAN, SHARD), jnp.bfloat16),
            pltpu.VMEM((SLOTS * SPAN, SHARD), jnp.bfloat16),
            pltpu.VMEM((ROWS, 2 * SHARD), jnp.float32),
            pltpu.SemaphoreType.DMA((2,)),
        ],
        compiler_params=pltpu.CompilerParams(vmem_limit_bytes=40 * 2**20),
        name="slot_grads",
    )(table, q_all, g_all, kv, all_stats)


def reduce_kernel(
    bg, enc_ref, kw_ref, vw_ref, dq_ref,
    dq_out, eg_out, kg_out, vg_out,
    enc, kw, vw, own_dq, zsb, zrb, csb, crb, xs1, xr1, xs2, xr2, group, ys1, yr1, ys2, yr2,
    local_sem, zs, zr, cs, cr, x1s, x1r, x2s, x2r, y1s, y1r, y2s, y2r,
):
    at = Place()
    out = Sends()
    bf16 = jnp.bfloat16

    loads = [
        pltpu.make_async_copy(enc_ref, enc, local_sem.at[0]),
        pltpu.make_async_copy(kw_ref, kw, local_sem.at[1]),
        pltpu.make_async_copy(vw_ref, vw, local_sem.at[2]),
    ]
    for copy in loads:
        copy.start()
    own_loads = []
    for j in range(ZN):
        own_loads.append(pltpu.make_async_copy(dq_ref.at[j * 2 + at.core], own_dq.at[j], local_sem.at[3 + j]))
        own_loads[-1].start()
    at.greet()

    order = (4, 3, -3, 2, -2, 1, -1, 0)

    def core_send(kind, which):
        target = wrap(at.z + order[which], ZN)
        device = (at.sibling, at.mp)
        src = dq_ref.at[target * 2 + 1 - at.core] if kind == 0 else csb.at[target]
        out.send(src, crb.at[kind, target], cs.at[kind, which], cr.at[kind, which], device)

    def weight_part(index):
        block = enc[index]
        return [dot(block, bg[:, col * SHARD : (col + 1) * SHARD], TN) for col in (0, 1)]

    def weight_for_sibling(which):
        target = wrap(at.z + order[which], ZN)
        parts = weight_part(target * 2 + 1 - at.core)
        for col in (0, 1):
            csb[target, pl.ds(col * HALF, HALF), :] = parts[col].astype(bf16)
        core_send(1, which)

    def term(kind, which, half):
        target = wrap(at.z + order[which], ZN)
        rows = pl.ds(half * HALF, HALF)
        if kind == 0:
            mine = own_dq[target, rows, :].astype(jnp.float32)
        else:
            mine = dot(enc[target * 2 + at.core], bg[:, half * SHARD : (half + 1) * SHARD], TN)
        return mine + crb[kind, target, rows, :].astype(jnp.float32)

    def z_region(step, way):
        return pl.ds(way * HALF, HALF) if step == 1 else pl.ds(0, ROWS)

    def z_step(kind, way, step):
        which = 0 if step == 1 else 2 * step - 3 + way
        target = wrap(at.z + order[which], ZN)
        if step > 1 or way == 0:
            landed(crb.at[kind, target], cr.at[kind, which])
        if step > 1:
            region = z_region(step - 1, way)
            landed(zrb.at[kind, way, step - 2, region], zr.at[kind, way, step - 2])
        for half in (0, 1):
            if step == 1 and half != way:
                continue
            rows = pl.ds(half * HALF, HALF)
            value = term(kind, which, half)
            if step > 2 or (step == 2 and half == way):
                value = value + zrb[kind, way, step - 2, rows, :].astype(jnp.float32)
            zsb[kind, way, step - 1, rows, :] = value.astype(bf16)
        region = z_region(step, way)
        out.send(
            zsb.at[kind, way, step - 1, region], zrb.at[kind, way, step - 1, region],
            zs.at[kind, way, step - 1], zr.at[kind, way, step - 1], at.z_device(way),
        )

    def z_final(kind):
        landed(crb.at[kind, at.z], cr.at[kind, 7])
        for way in (0, 1):
            landed(zrb.at[kind, way, 3], zr.at[kind, way, 3])
        for half in (0, 1):
            rows = pl.ds(half * HALF, HALF)
            value = term(kind, 7, half)
            for way in (0, 1):
                value = value + zrb[kind, way, 3, rows, :].astype(jnp.float32)
            if kind == 0:
                dq_out[rows, :] = value.astype(bf16)
            elif half == 0:
                kg_out[...] = value
            else:
                vg_out[...] = value

    def width_index(path, offset, j):
        if path == 0:
            return wrap(at.x + offset, SIDE) * SIDE + j
        return j * SIDE + wrap(at.y + offset, SIDE)

    def width_part(path, start, size, offset, j):
        rows = pl.ds(path * HALF + start, size)
        cols = pl.ds(pl.multiple_of(width_index(path, offset, j) * SHARD, SHARD), SHARD)
        return dot(bg[rows, :SHARD], kw[cols, :], NT) + dot(bg[rows, SHARD:], vw[cols, :], NT)

    def width_far(path):
        def one(j, carry):
            value = width_part(path, 0, HALF, 2, j).astype(bf16)
            for way in (0, 1):
                xs1[path, way, j] = value[way * CHUNK : (way + 1) * CHUNK, :]
            return carry

        lax.fori_loop(0, SIDE, one, 0)
        for way in (0, 1):
            device = (at.dp, at.plane_neighbour(path, 0, way))
            out.send(xs1.at[path, way], xr1.at[path, way], x1s.at[path, way], x1r.at[path, way], device)

    def width_near(path, way):
        landed(xr1.at[path, way], x1r.at[path, way])

        def one(j, carry):
            value = width_part(path, 0, HALF, 1 if way == 0 else -1, j)
            came = xr1[path, way, j].astype(jnp.float32)
            for part in (0, 1):
                piece = value[part * CHUNK : (part + 1) * CHUNK, :]
                piece = piece + came if part == way else piece
                xs2[path, way, j, pl.ds(part * CHUNK, CHUNK), :] = piece.astype(bf16)
            return carry

        lax.fori_loop(0, SIDE, one, 0)
        device = (at.dp, at.plane_neighbour(path, 0, way))
        out.send(xs2.at[path, way], xr2.at[path, way], x2s.at[path, way], x2r.at[path, way], device)

    def second(path):
        return at.y if path == 0 else at.x

    def width_own(path):
        for way in (0, 1):
            landed(xr2.at[path, way], x2r.at[path, way])

        def one(j, carry):
            value = width_part(path, 0, HALF, 0, j)
            for way in (0, 1):
                value = value + xr2[path, way, j].astype(jnp.float32)
            group[path, j] = value
            return carry

        lax.fori_loop(0, SIDE, one, 0)
        far = wrap(second(path) + 2, SIDE)
        for way in (0, 1):
            ys1[path, way] = group[path, far, pl.ds(way * CHUNK, CHUNK), :].astype(bf16)
            device = (at.dp, at.plane_neighbour(path, 1, way))
            out.send(ys1.at[path, way], yr1.at[path, way], y1s.at[path, way], y1r.at[path, way], device)

    def width_second(path):
        for way in (0, 1):
            landed(yr1.at[path, way], y1r.at[path, way])
            near = wrap(second(path) + (1 if way == 0 else -1), SIDE)
            for part in (0, 1):
                piece = group[path, near, pl.ds(part * CHUNK, CHUNK), :]
                if part == way:
                    piece = piece + yr1[path, way].astype(jnp.float32)
                ys2[path, way, pl.ds(part * CHUNK, CHUNK), :] = piece.astype(bf16)
            device = (at.dp, at.plane_neighbour(path, 1, way))
            out.send(ys2.at[path, way], yr2.at[path, way], y2s.at[path, way], y2r.at[path, way], device)

    def width_final(path):
        value = group[path, second(path)]
        for way in (0, 1):
            landed(yr2.at[path, way], y2r.at[path, way])
            value = value + yr2[path, way].astype(jnp.float32)
        eg_out[pl.ds(path * HALF, HALF), :] = value.astype(bf16)

    for which in range(ZN):
        core_send(0, which)
    loads[0].wait()
    weight_for_sibling(0)
    for copy in own_loads:
        copy.wait()
    for way in (0, 1):
        z_step(0, way, 1)
    loads[1].wait()
    loads[2].wait()
    for path in (0, 1):
        width_far(path)
    for way in (0, 1):
        z_step(1, way, 1)
    weight_for_sibling(1)
    weight_for_sibling(2)
    for way in (0, 1):
        z_step(0, way, 2)
    for way in (0, 1):
        for path in (0, 1):
            width_near(path, way)
    for way in (0, 1):
        z_step(1, way, 2)
    weight_for_sibling(3)
    weight_for_sibling(4)
    for way in (0, 1):
        z_step(0, way, 3)
    for path in (0, 1):
        width_own(path)
    for way in (0, 1):
        z_step(1, way, 3)
    for which in (5, 6, 7):
        weight_for_sibling(which)
    for path in (0, 1):
        width_second(path)
    for way in (0, 1):
        z_step(0, way, 4)
    for path in (0, 1):
        width_final(path)
    for way in (0, 1):
        z_step(1, way, 4)
    z_final(0)
    z_final(1)
    out.finish()


def reduce_all(block_grad, enc_all, key_weight, value_weight, dq):
    any_ = pl.BlockSpec(memory_space=pl.ANY)
    vmem = pl.BlockSpec(memory_space=pltpu.VMEM)
    dma = pltpu.SemaphoreType.DMA
    bf16, f32 = jnp.bfloat16, jnp.float32
    return pl.pallas_call(
        reduce_kernel,
        out_shape=(
            jax.ShapeDtypeStruct((ROWS, SHARD), bf16),
            jax.ShapeDtypeStruct((ROWS, SHARD), bf16),
            jax.ShapeDtypeStruct((SHARD, SHARD), f32),
            jax.ShapeDtypeStruct((SHARD, SHARD), f32),
        ),
        in_specs=[vmem, any_, any_, any_, any_],
        out_specs=(vmem, vmem, vmem, vmem),
        scratch_shapes=[
            pltpu.VMEM((MP, ROWS, SHARD), bf16),
            pltpu.VMEM((MP * SHARD, SHARD), bf16),
            pltpu.VMEM((MP * SHARD, SHARD), bf16),
            pltpu.VMEM((ZN, ROWS, SHARD), bf16),
            pltpu.VMEM((2, 2, 4, ROWS, SHARD), bf16),
            pltpu.VMEM((2, 2, 4, ROWS, SHARD), bf16),
            pltpu.VMEM((ZN, ROWS, SHARD), bf16),
            pltpu.VMEM((2, ZN, ROWS, SHARD), bf16),
            pltpu.VMEM((2, 2, SIDE, CHUNK, SHARD), bf16),
            pltpu.VMEM((2, 2, SIDE, CHUNK, SHARD), bf16),
            pltpu.VMEM((2, 2, SIDE, HALF, SHARD), bf16),
            pltpu.VMEM((2, 2, SIDE, HALF, SHARD), bf16),
            pltpu.VMEM((2, SIDE, HALF, SHARD), f32),
            pltpu.VMEM((2, 2, CHUNK, SHARD), bf16),
            pltpu.VMEM((2, 2, CHUNK, SHARD), bf16),
            pltpu.VMEM((2, 2, HALF, SHARD), bf16),
            pltpu.VMEM((2, 2, HALF, SHARD), bf16),
            dma((3 + ZN,)),
            dma((2, 2, 4)), dma((2, 2, 4)),
            dma((2, ZN)), dma((2, ZN)),
            dma((2, 2)), dma((2, 2)),
            dma((2, 2)), dma((2, 2)),
            dma((2, 2)), dma((2, 2)),
            dma((2, 2)), dma((2, 2)),
        ],
        compiler_params=pltpu.CompilerParams(
            collective_id=2, has_side_effects=True, vmem_limit_bytes=56 * 2**20
        ),
        name="reduce_all",
    )(block_grad, enc_all, key_weight, value_weight, dq)


def slot_table(ids_all):
    ids = ids_all[:, :, :K].reshape(DP, DP)
    me = lax.axis_index("dp")
    owners, local_block = ids // NB_DEV, ids % NB_DEV
    position = jnp.arange(DP, dtype=jnp.int32)
    alike = (owners[:, :, None] == owners[:, None, :]) & (position[None, :] < position[:, None])
    ranks = jnp.sum(alike.astype(jnp.int32), axis=-1)

    def other(values):
        return values.reshape(DP, DP // K, K)[:, :, ::-1].reshape(DP, DP)

    matched = (owners == me)[:, :, None] & (ranks[:, :, None] == jnp.arange(2, dtype=jnp.int32))
    columns = [
        jnp.broadcast_to(position // K, (DP, DP)), local_block,
        other(owners), other(ranks), jnp.ones((DP, DP), jnp.int32),
    ]
    picked = [jnp.sum(jnp.where(matched, c[:, :, None], 0), axis=1).reshape(-1) for c in columns]
    return jnp.concatenate(picked + [jnp.full((32,), me, jnp.int32)])


def body(queries, grad_attn, encoded, key_weight, value_weight, nbr_ids):
    ids = jnp.pad(nbr_ids, ((0, 0), (0, 128 - K)))
    q_all, g_all, enc_all, kv, ids_all = gather(
        queries, grad_attn, encoded, ids, key_weight, value_weight
    )
    table = slot_table(ids_all)
    stats = slot_stats(table, q_all, g_all, kv)
    all_stats = share_stats(stats)
    block_grad, dq = slot_grads(table, q_all, g_all, kv, all_stats)
    return reduce_all(block_grad, enc_all, key_weight, value_weight, dq)


def solution(mesh):
    return jax.shard_map(
        body,
        mesh=mesh,
        in_specs=(
            P("dp", "mp"),
            P("dp", "mp"),
            P("dp", "mp"),
            P(None, "mp"),
            P(None, "mp"),
            P("dp", None),
        ),
        out_specs=(P("dp", "mp"), P("dp", "mp"), P("dp", "mp"), P("dp", "mp")),
        check_vma=False,
    )
```

```python
import math

import jax
import jax.numpy as jnp
from jax import lax
from jax.experimental import pallas as pl
from jax.experimental.pallas import tpu as pltpu
from jax.sharding import PartitionSpec as P

HD = 128
SPAN = 64
NL = 128
K = 2
NB_DEV = 4
HEADS = 2
DP = 16
MP = 16
ZN = 8
SIDE = 4
SHARD = 256
ROWS = 512
HALF = 256
CHUNK = 128
PAIR = 2 * SPAN
MESH = pl.DeviceIdType.MESH
SCALE = 1.0 / math.sqrt(HD)
OFFSETS = (0, -1, 1, 2)
SPAN_MASK = 7
RING = (4, 3, -3, 2, -2, 1, -1, 0)
NT = (((1,), (1,)), ((), ()))
NN = (((1,), (0,)), ((), ()))
TN = (((0,), (0,)), ((), ()))
BF16, F32, I32 = jnp.bfloat16, jnp.float32, jnp.int32


def dot(a, b, dims):
    return lax.dot_general(a, b, dims, preferred_element_type=F32)


def wrap(value, size):
    return lax.rem(value + size, size)


class Place:
    def __init__(self):
        self.dp = lax.axis_index("dp")
        self.mp = lax.axis_index("mp")
        self.z, self.core = lax.div(self.dp, 2), lax.rem(self.dp, 2)
        self.x, self.y = lax.div(self.mp, SIDE), lax.rem(self.mp, SIDE)
        self.sibling = self.z * 2 + 1 - self.core

    def along_z(self, step, other_core=False):
        core = 1 - self.core if other_core else self.core
        return wrap(self.z + step, ZN) * 2 + core

    def in_plane(self, path, first, second):
        along_x, along_y = (first, second) if path == 0 else (second, first)
        return wrap(self.x + along_x, SIDE) * SIDE + wrap(self.y + along_y, SIDE)

    def plane_neighbour(self, path, axis, way):
        step = 1 if way == 0 else -1
        return self.in_plane(path, step, 0) if axis == 0 else self.in_plane(path, 0, step)

    def z_device(self, way):
        return (self.along_z(1 if way == 0 else -1), self.mp)

    def greet(self):
        barrier = pltpu.get_barrier_semaphore()
        others = [(wrap(self.dp + k, DP), self.mp) for k in range(1, DP)]
        others += [(self.dp, self.plane_neighbour(0, axis, way)) for axis in (0, 1) for way in (0, 1)]
        for device in others:
            pl.semaphore_signal(barrier, inc=1, device_id=device, device_id_type=MESH)
        pl.semaphore_wait(barrier, len(others))


def send(src, dst, send_sem, recv_sem, device):
    pltpu.make_async_remote_copy(
        src_ref=src,
        dst_ref=dst,
        send_sem=send_sem,
        recv_sem=recv_sem,
        device_id=device,
        device_id_type=MESH,
    ).start()


def landed(ref, sem):
    pltpu.make_async_copy(ref, ref, sem).wait()


def kernel(
    ids_ref, q_ref, g_ref, e_ref, kw_ref, vw_ref,
    dq_out, eg_out, kg_out, vg_out,
    q_all, g_all, ids_all, tab, enc, w, acc, kv, kt, q_sel, g_sel, score_sv, pgrad_sv, st_own, st_all,
    dqs, dqr, bg, csb, crb, zsb, zrb, xs1, xr1, xs2, xr2, group, ys1, yr1, ys2, yr2,
    local_sem, sent, zr, cr, ir, icr, p1r, p1f, p2r, p2f, sr, scr, dqrs, wcr, wzr, x1r, x2r, y1r, y2r,
):
    at = Place()
    here = (at.sibling, at.mp)
    srcs, alls = (q_ref, g_ref), (q_all, g_all)
    own_cols = [slice(h * HD, (h + 1) * HD) for h in range(HEADS)]

    ids_all[at.dp] = ids_ref[...]
    at.greet()

    def z_send(way, step, kind, h):
        origin = at.along_z(1 - step if way == 0 else step - 1)
        dst = alls[kind].at[h, origin]
        src = srcs[kind].at[:, own_cols[h]] if step == 1 else dst
        send(src, dst, sent.at[h], zr.at[h, kind, way, step - 1], at.z_device(way))

    def core_send(which, kind, h, origin):
        dst = alls[kind].at[h, origin]
        src = srcs[kind].at[:, own_cols[h]] if which == 0 else dst
        distance = which if which < 5 else which - 4
        send(src, dst, sent.at[2 + h], cr.at[h, max(distance - 2, 0)], here)

    def carries(way, step, kind):
        return step < 4 or (step == 4 and way == kind)

    def z_arrive(step, h):
        for kind in (0, 1):
            for way in (0, 1):
                if not carries(way, step, kind):
                    continue
                origin = at.along_z(-step if way == 0 else step)
                landed(alls[kind].at[h, origin], zr.at[h, kind, way, step - 1])
                if carries(way, step + 1, kind):
                    z_send(way, step + 1, kind, h)
                core_send(way * 4 + step, kind, h, origin)

    def z_start(h):
        for kind in (0, 1):
            for way in (0, 1):
                z_send(way, 1, kind, h)
        for kind in (0, 1):
            core_send(0, kind, h, at.dp)

    def core_arrived(h, near):
        landed(q_all.at[h, pl.ds(0, (10, 4, 2)[near])], cr.at[h, near])

    def ids_send(way, step):
        block = ids_all.at[at.along_z(1 - step if way == 0 else step - 1)]
        send(block, block, sent.at[4], ir.at[way, step - 1], at.z_device(way))

    def ids_core(origin):
        block = ids_all.at[origin]
        send(block, block, sent.at[5], icr.at[0], here)

    def ids_arrive(step):
        for way in (0, 1):
            if step == 4 and way == 1:
                continue
            origin = at.along_z(-step if way == 0 else step)
            landed(ids_all.at[origin], ir.at[way, step - 1])
            if step < 3 or (step == 3 and way == 0):
                ids_send(way, step + 1)
            ids_core(origin)

    def lane_sum(value):
        for hop in (64, 32, 16, 8, 4, 2, 1):
            value = value + pltpu.roll(value, hop, 1)
        return value

    def make_tables():
        landed(ids_all.at[pl.ds(0, ZN)], icr.at[0])
        ids = ids_all[:, 0, :]
        slot = lax.broadcasted_iota(I32, (DP, 128), 1)
        owners = jnp.right_shift(ids, 2)
        ranks = jnp.zeros((DP, 128), I32)
        for back in range(1, DP):
            same = (pltpu.roll(owners, back, 1) == owners) & (slot >= back)
            ranks = ranks + jnp.where(same, 1, 0)
        places = owners * 2 + ranks
        even = jnp.bitwise_and(slot, 1) == 0
        partner = jnp.where(even, pltpu.roll(places, 127, 1), pltpu.roll(places, 1, 1))
        code = jnp.right_shift(slot, 1) + 8 * jnp.bitwise_and(ids, 3) + 32 * partner + 1024
        for rank in (0, 1):
            mine = (owners == at.dp) & (ranks == rank) & (slot < DP)
            tab[rank] = lane_sum(jnp.where(mine, code, 0))
        tab[2] = jnp.where(slot < SPAN, tab[0], tab[1])
        tab[3] = places
        own = tab[3, pl.ds(at.dp, 1), :]
        diagonal = slot == lax.broadcasted_iota(I32, (DP, 128), 0)
        tab[3] = lane_sum(jnp.where(diagonal, own, 0))

    def rows_of(path):
        return pl.ds(path * HALF, HALF)

    def part_of(path, way):
        return pl.ds(path * HALF + way * CHUNK, CHUNK)

    def p2_first(path, k):
        origin = at.in_plane(path, OFFSETS[k], 0)
        dst = enc.at[origin, rows_of(path)]
        src = e_ref.at[rows_of(path)] if k == 0 else dst
        for way in (0, 1):
            device = (at.dp, at.plane_neighbour(path, 1, way))
            send(src, dst, sent.at[7], p2r.at[path, k, way], device)

    def p1_first(path):
        for way in (0, 1):
            device = (at.dp, at.plane_neighbour(path, 0, way))
            send(
                e_ref.at[rows_of(path)], enc.at[at.mp, rows_of(path)],
                sent.at[6], p1r.at[path, way], device,
            )

    def p1_arrive(path, way):
        origin = at.in_plane(path, -1 if way == 0 else 1, 0)
        landed(enc.at[origin, rows_of(path)], p1r.at[path, way])
        part = enc.at[origin, part_of(path, way)]
        device = (at.dp, at.plane_neighbour(path, 0, way))
        send(part, part, sent.at[6], p1f.at[path], device)
        p2_first(path, 1 + way)

    def p1_far(path):
        landed(enc.at[at.in_plane(path, 2, 0), rows_of(path)], p1f.at[path])
        p2_first(path, 3)

    def p2_arrive(path, k):
        for way in (0, 1):
            origin = at.in_plane(path, OFFSETS[k], -1 if way == 0 else 1)
            landed(enc.at[origin, rows_of(path)], p2r.at[path, k, way])
            part = enc.at[origin, part_of(path, way)]
            device = (at.dp, at.plane_neighbour(path, 1, way))
            send(part, part, sent.at[7], p2f.at[0], device)

    def p2_far():
        landed(enc.at[pl.ds(0, SIDE)], p2f.at[0])

    def project(h):
        def one(j, total):
            for k in range(SIDE):
                rows = pl.ds(pl.multiple_of((j * SIDE + k) * SHARD, SHARD), SHARD)
                part = dot(enc[j * SIDE + k], w[h, rows, :], NN)
                total = part if k == 0 else total + part
            acc[...] += total
            return total

        acc[...] = jnp.zeros_like(acc)
        lax.fori_loop(0, SIDE, lambda j, c: (one(j, None), c)[1], 0)
        kv[h] = acc[...].astype(BF16)
        kt[h] = jnp.transpose(kv[h, :, :HD])

    low = lax.broadcasted_iota(I32, (1, PAIR), 1) < SPAN

    def chosen(ref, h, i):
        picked = []
        for rank in (0, 1):
            span = jnp.bitwise_and(tab[rank, pl.ds(i, 1), :], SPAN_MASK)
            total = None
            for s in range(ROWS // SPAN):
                factor = jnp.where(span == s, 1.0, 0.0).astype(BF16)
                term = ref[h, i, pl.ds(s * SPAN, SPAN), :] * factor
                total = term if total is None else total + term
            picked.append(total)
        return jnp.concatenate(picked, axis=0)

    def lane_codes(chip):
        return jnp.concatenate([tab[2, pl.ds(chip * 2 + core, 1), :] for core in (0, 1)], axis=1)

    def blocks_of(codes):
        return jnp.bitwise_and(jnp.right_shift(codes, 3), 3)

    def chip_stats(h, chip):
        block = blocks_of(lane_codes(chip))
        for ref, sel in ((q_all, q_sel), (g_all, g_sel)):
            for core in (0, 1):
                sel[h, chip, pl.ds(core * PAIR, PAIR), :] = chosen(ref, h, chip * 2 + core)
        qh, gh = q_sel[h, chip], g_sel[h, chip]
        scores = pgrad = None
        for b in range(NB_DEV):
            rows = pl.ds(b * NL, NL)
            s = dot(kv[h, rows, :HD], qh, NT)
            p = dot(kv[h, rows, HD:], gh, NT)
            scores = s if b == 0 else jnp.where(block == b, s, scores)
            pgrad = p if b == 0 else jnp.where(block == b, p, pgrad)
        scores = scores * SCALE
        top = jnp.max(scores, axis=0, keepdims=True)
        e = jnp.exp(scores - top)
        total = jnp.sum(e, axis=0, keepdims=True)
        lse = top + jnp.log(total)
        delta = jnp.sum(e * pgrad, axis=0, keepdims=True) / total
        for core in (0, 1):
            lanes = slice(core * PAIR, (core + 1) * PAIR)
            st_own[h, pl.ds(chip * 4 + core * 2, 1), :] = lse[:, lanes]
            st_own[h, pl.ds(chip * 4 + core * 2 + 1, 1), :] = delta[:, lanes]
        score_sv[h, chip] = scores
        pgrad_sv[h, chip] = pgrad

    def stats(h, near):
        first, step, count = ((6, 1, 5), (3, 2, 2), (4, 1, 1))[near]

        def one(t, carry):
            chip_stats(h, lax.rem(at.z + first + step * t, ZN))
            return carry

        lax.fori_loop(0, count, one, 0)

    def stats_send(h):
        for k in (4, 3, 5, 2, 6, 1, 7):
            device = (at.along_z(k), at.mp)
            send(st_own.at[h], st_all.at[h, at.dp], sent.at[8 + h], sr.at[h, at.z], device)
        send(st_own.at[h], st_all.at[h, at.dp], sent.at[10 + h], scr.at[h], here)

    def stats_forward(h):
        for k in (1, 7, 2, 6, 3, 5, 4):
            origin = at.along_z(k)
            landed(st_all.at[h, origin], sr.at[h, wrap(at.z + k, ZN)])
            send(st_all.at[h, origin], st_all.at[h, origin], sent.at[10 + h], scr.at[h], here)

    def stats_arrived(h):
        landed(st_all.at[h, pl.ds(0, ZN)], scr.at[h])
        st_all[h, at.dp] = st_own[h]

    def merged(h, i):
        code = tab[2, pl.ds(i, 1), :]
        partner = jnp.bitwise_and(jnp.right_shift(code, 5), 31)
        owner = jnp.right_shift(partner, 1)
        turned = pltpu.roll(owner, SPAN, 1)
        straight = jnp.zeros((2, PAIR), F32)
        crossed = jnp.zeros((2, PAIR), F32)
        for o in range(DP):
            pair = st_all[h, o, pl.ds(i * 2, 2), :]
            straight = jnp.where(owner == o, pair, straight)
            crossed = jnp.where(turned == o, pair, crossed)
        same = (jnp.bitwise_and(partner, 1) == 0) == low
        there = jnp.where(same, straight, pltpu.roll(crossed, SPAN, 1))
        own = st_own[h, pl.ds(i * 2, 2), :]
        lse_here, lse_there = own[:1], there[:1]
        top = jnp.maximum(lse_here, lse_there)
        lse = top + jnp.log(jnp.exp(lse_here - top) + jnp.exp(lse_there - top))
        delta = jnp.exp(lse_here - lse) * own[1:] + jnp.exp(lse_there - lse) * there[1:]
        return lse, delta

    def chip_grads(h, chip):
        codes = lane_codes(chip)
        block = jnp.where(jnp.right_shift(codes, 10) > 0, blocks_of(codes), NB_DEV)
        parts = [merged(h, chip * 2 + core) for core in (0, 1)]
        lse = jnp.concatenate([p[0] for p in parts], axis=1)
        delta = jnp.concatenate([p[1] for p in parts], axis=1)
        prob = jnp.exp(score_sv[h, chip] - lse)
        score_grad = prob * (pgrad_sv[h, chip] - delta) * SCALE
        zero = jnp.zeros_like(prob)
        prob_by_block = jnp.concatenate(
            [jnp.where(block == b, prob, zero).astype(BF16) for b in range(NB_DEV)], axis=0
        )
        grad_by_block = jnp.concatenate(
            [jnp.where(block == b, score_grad, zero).astype(BF16) for b in range(NB_DEV)], axis=0
        )
        acc[:, :HD] += dot(grad_by_block, q_sel[h, chip], NN)
        acc[:, HD:] += dot(prob_by_block, g_sel[h, chip], NN)
        dq = jnp.transpose(dot(kt[h], grad_by_block, NN)).astype(BF16)
        for core in (0, 1):
            dqs[h, chip * 2 + core] = dq[core * PAIR : (core + 1) * PAIR, :]

    def grads(h):
        acc[...] = jnp.zeros_like(acc)

        def one(chip, carry):
            chip_grads(h, chip)
            return carry

        lax.fori_loop(0, ZN, one, 0)
        dqr[h, at.dp] = dqs[h, at.dp]
        bg[h] = acc[...].astype(BF16)

    def dq_send(h, begin, end):
        def one(k, carry):
            i = wrap(at.dp + k, DP)
            send(dqs.at[h, i], dqr.at[h, at.dp], sent.at[12 + h], dqrs.at[h], (i, at.mp))
            return carry

        lax.fori_loop(begin, end, one, 0)

    def dq_final(h):
        landed(dqr.at[h, pl.ds(0, DP - 1)], dqrs.at[h])

        def one(c, carry):
            places = [tab[3, pl.ds(c * K + k, 1), :] for k in range(K)]
            total = jnp.zeros((SPAN, HD), BF16)
            for m in range(2 * DP):
                hit = (places[0] == m) | (places[1] == m)
                factor = jnp.where(hit, 1.0, 0.0).astype(BF16)
                total = total + dqr[h, m // 2, pl.ds(m % 2 * SPAN, SPAN), :] * factor
            dq_out[pl.ds(pl.multiple_of(c * SPAN, SPAN), SPAN), own_cols[h]] = total
            return carry

        lax.fori_loop(0, ROWS // SPAN, one, 0)

    def weight_sibling(h, begin, end):
        def one(which, carry):
            near = lax.div(which + 1, 2)
            sign = 2 * lax.rem(which, 2) - 1
            target = wrap(at.z + sign * (4 - near), ZN)
            csb[h, target] = dot(enc[target * 2 + 1 - at.core], bg[h], TN).astype(BF16)
            send(csb.at[h, target], crb.at[h, target], sent.at[14 + h], wcr.at[h, near], here)
            return carry

        lax.fori_loop(begin, end, one, 0)

    def weight_met(h, near):
        landed(crb.at[h, pl.ds(0, 1 if near in (0, 4) else 2)], wcr.at[h, near])

    def weight_term(h, which):
        target = wrap(at.z + RING[which], ZN)
        return dot(enc[target * 2 + at.core], bg[h], TN) + crb[h, target].astype(F32)

    def z_region(step, way):
        return pl.ds(way * CHUNK, CHUNK) if step == 1 else pl.ds(0, SHARD)

    def weight_put(h, way, step, value):
        region = z_region(step, way)
        zsb[h, way, step - 1, region, :] = value.astype(BF16)
        send(
            zsb.at[h, way, step - 1, region], zrb.at[h, way, step - 1, region],
            sent.at[16 + h], wzr.at[h, way, step - 1], at.z_device(way),
        )

    def weight_step(h, step):
        if step == 1:
            weight_met(h, 0)
            value = weight_term(h, 0)
            for way in (0, 1):
                weight_put(h, way, 1, value[way * CHUNK : (way + 1) * CHUNK, :])
            return
        weight_met(h, step - 1)
        for way in (0, 1):
            which = 2 * step - 3 + way
            value = weight_term(h, which)
            region = z_region(step - 1, way)
            landed(zrb.at[h, way, step - 2, region], wzr.at[h, way, step - 2])
            came = zrb[h, way, step - 2, region, :].astype(F32)
            if step == 2:
                pieces = [value[:CHUNK, :], value[CHUNK:, :]]
                pieces[way] = pieces[way] + came
                value = jnp.concatenate(pieces, axis=0)
            else:
                value = value + came
            weight_put(h, way, step, value)

    def weight_final(h):
        weight_met(h, 4)
        value = weight_term(h, 7)
        for way in (0, 1):
            landed(zrb.at[h, way, 3], wzr.at[h, way, 3])
            value = value + zrb[h, way, 3].astype(F32)
        kg_out[:, own_cols[h]] = value[:, :HD]
        vg_out[:, own_cols[h]] = value[:, HD:]

    def width_part(path, offset, j):
        if path == 0:
            index = wrap(at.x + offset, SIDE) * SIDE + j
        else:
            index = j * SIDE + wrap(at.y + offset, SIDE)
        cols = pl.ds(pl.multiple_of(index * SHARD, SHARD), SHARD)
        return sum(dot(bg[h, rows_of(path), :], w[h, cols, :], NT) for h in range(HEADS))

    def width_far(path):
        def one(j, carry):
            value = width_part(path, 2, j).astype(BF16)
            for way in (0, 1):
                xs1[path, way, j] = value[way * CHUNK : (way + 1) * CHUNK, :]
            return carry

        lax.fori_loop(0, SIDE, one, 0)
        for way in (0, 1):
            device = (at.dp, at.plane_neighbour(path, 0, way))
            send(xs1.at[path, way], xr1.at[path, way], sent.at[18], x1r.at[path, way], device)

    def width_near(path, way):
        landed(xr1.at[path, way], x1r.at[path, way])

        def one(j, carry):
            value = width_part(path, 1 if way == 0 else -1, j)
            came = xr1[path, way, j].astype(F32)
            for part in (0, 1):
                piece = value[part * CHUNK : (part + 1) * CHUNK, :]
                piece = piece + came if part == way else piece
                xs2[path, way, j, pl.ds(part * CHUNK, CHUNK), :] = piece.astype(BF16)
            return carry

        lax.fori_loop(0, SIDE, one, 0)
        device = (at.dp, at.plane_neighbour(path, 0, way))
        send(xs2.at[path, way], xr2.at[path, way], sent.at[19], x2r.at[path], device)

    def second(path):
        return at.y if path == 0 else at.x

    def width_own(path):
        landed(xr2.at[path], x2r.at[path])

        def one(j, carry):
            value = width_part(path, 0, j)
            for way in (0, 1):
                value = value + xr2[path, way, j].astype(F32)
            group[path, j] = value
            return carry

        lax.fori_loop(0, SIDE, one, 0)
        far = wrap(second(path) + 2, SIDE)
        for way in (0, 1):
            ys1[path, way] = group[path, far, pl.ds(way * CHUNK, CHUNK), :].astype(BF16)
            device = (at.dp, at.plane_neighbour(path, 1, way))
            send(ys1.at[path, way], yr1.at[path, way], sent.at[20], y1r.at[path, way], device)

    def width_second(path):
        for way in (0, 1):
            landed(yr1.at[path, way], y1r.at[path, way])
            near = wrap(second(path) + (1 if way == 0 else -1), SIDE)
            for part in (0, 1):
                piece = group[path, near, pl.ds(part * CHUNK, CHUNK), :]
                if part == way:
                    piece = piece + yr1[path, way].astype(F32)
                ys2[path, way, pl.ds(part * CHUNK, CHUNK), :] = piece.astype(BF16)
            device = (at.dp, at.plane_neighbour(path, 1, way))
            send(ys2.at[path, way], yr2.at[path, way], sent.at[21], y2r.at[path], device)

    def width_final(path):
        value = group[path, second(path)]
        landed(yr2.at[path], y2r.at[path])
        for way in (0, 1):
            value = value + yr2[path, way].astype(F32)
        eg_out[pl.ds(path * HALF, HALF), :] = value.astype(BF16)

    def finish():
        for h in range(HEADS):
            landed(q_all.at[h, pl.ds(0, 14)], sent.at[h])
            landed(q_all.at[h], sent.at[2 + h])
            landed(st_all.at[h, pl.ds(0, ZN - 1)], sent.at[8 + h])
            landed(st_all.at[h, pl.ds(0, ZN)], sent.at[10 + h])
            landed(dqr.at[h, pl.ds(0, DP - 1)], sent.at[12 + h])
            landed(crb.at[h], sent.at[14 + h])
            landed(crb.at[h, pl.ds(0, 7)], sent.at[16 + h])
        landed(ids_all.at[pl.ds(0, 7)], sent.at[4])
        landed(ids_all.at[pl.ds(0, ZN)], sent.at[5])
        landed(enc.at[pl.ds(0, 3)], sent.at[6])
        landed(enc.at[pl.ds(0, 12)], sent.at[7])
        for n, ref in enumerate((xr1, xr2, yr1, yr2)):
            landed(ref, sent.at[18 + n])

    for way in (0, 1):
        ids_send(way, 1)
    z_start(0)
    ids_core(at.dp)
    for path in (0, 1):
        p1_first(path)
    for path in (0, 1):
        p2_first(path, 0)
    pltpu.make_async_copy(e_ref, enc.at[at.mp], local_sem.at[0]).start()
    for h in range(HEADS):
        cols = own_cols[h]
        pltpu.make_async_copy(q_ref.at[:, cols], q_all.at[h, at.dp], local_sem.at[1]).start()
        pltpu.make_async_copy(g_ref.at[:, cols], g_all.at[h, at.dp], local_sem.at[1]).start()
        pltpu.make_async_copy(kw_ref.at[:, cols], w.at[h, :, pl.ds(0, HD)], local_sem.at[2]).start()
        pltpu.make_async_copy(vw_ref.at[:, cols], w.at[h, :, pl.ds(HD, HD)], local_sem.at[2]).start()

    for way in (0, 1):
        for path in (0, 1):
            p1_arrive(path, way)
    ids_arrive(1)
    for path in (0, 1):
        p2_arrive(path, 0)
    z_arrive(1, 0)
    for path in (0, 1):
        p1_far(path)
    ids_arrive(2)
    for path in (0, 1):
        p2_arrive(path, 1)
    z_arrive(2, 0)
    z_start(1)
    for path in (0, 1):
        p2_arrive(path, 2)
    ids_arrive(3)
    for path in (0, 1):
        p2_arrive(path, 3)
    z_arrive(3, 0)
    ids_arrive(4)
    p2_far()
    landed(enc.at[0], local_sem.at[0])
    landed(q_all.at[0, pl.ds(0, 4)], local_sem.at[1])
    landed(w, local_sem.at[2])
    make_tables()
    z_arrive(1, 1)
    project(0)
    core_arrived(0, 0)
    stats(0, 0)
    z_arrive(4, 0)
    z_arrive(2, 1)
    core_arrived(0, 1)
    stats(0, 1)
    core_arrived(0, 2)
    stats(0, 2)
    stats_send(0)
    project(1)
    z_arrive(3, 1)
    stats_forward(0)
    core_arrived(1, 0)
    stats(1, 0)
    stats_arrived(0)
    grads(0)
    z_arrive(4, 1)
    core_arrived(1, 1)
    stats(1, 1)
    core_arrived(1, 2)
    stats(1, 2)
    stats_send(1)
    dq_send(0, 1, DP)
    weight_sibling(0, 0, 3)
    weight_step(0, 1)
    stats_forward(1)
    weight_sibling(0, 3, 8)
    weight_step(0, 2)
    stats_arrived(1)
    grads(1)
    weight_sibling(1, 0, 3)
    weight_step(1, 1)
    dq_send(1, 1, DP)
    weight_step(0, 3)
    for path in (0, 1):
        width_far(path)
    weight_sibling(1, 3, 8)
    weight_step(1, 2)
    weight_step(0, 4)
    for path in (0, 1):
        width_near(path, 0)
    weight_step(1, 3)
    for path in (0, 1):
        width_near(path, 1)
    weight_final(0)
    for path in (0, 1):
        width_own(path)
    weight_step(1, 4)
    dq_final(0)
    for path in (0, 1):
        width_second(path)
    for path in (0, 1):
        width_final(path)
    dq_final(1)
    weight_final(1)
    finish()


def publish_kernel(a, b, c, d, a_out, b_out, c_out, d_out):
    for src, dst in ((a, a_out), (b, b_out), (c, c_out), (d, d_out)):
        dst[...] = src[...]


def body(queries, grad_attn, encoded, key_weight, value_weight, nbr_ids):
    hbm = pl.BlockSpec(memory_space=pltpu.HBM)
    vmem = pl.BlockSpec(memory_space=pltpu.VMEM)
    dma = pltpu.SemaphoreType.DMA
    shapes = (
        jax.ShapeDtypeStruct((ROWS, SHARD), BF16),
        jax.ShapeDtypeStruct((ROWS, SHARD), BF16),
        jax.ShapeDtypeStruct((SHARD, SHARD), F32),
        jax.ShapeDtypeStruct((SHARD, SHARD), F32),
    )
    ids = jnp.pad(nbr_ids.reshape(1, DP), ((0, 7), (0, 128 - DP)))
    results = pl.pallas_call(
        kernel,
        out_shape=shapes,
        in_specs=[vmem] + [hbm] * 5,
        out_specs=(vmem, vmem, vmem, vmem),
        scratch_shapes=[
            pltpu.VMEM((HEADS, DP, ROWS, HD), BF16),
            pltpu.VMEM((HEADS, DP, ROWS, HD), BF16),
            pltpu.VMEM((DP, 8, 128), I32),
            pltpu.VMEM((4, DP, 128), I32),
            pltpu.VMEM((MP, ROWS, SHARD), BF16),
            pltpu.VMEM((HEADS, MP * SHARD, 2 * HD), BF16),
            pltpu.VMEM((ROWS, 2 * HD), F32),
            pltpu.VMEM((HEADS, ROWS, 2 * HD), BF16),
            pltpu.VMEM((HEADS, HD, ROWS), BF16),
            pltpu.VMEM((HEADS, ZN, 2 * PAIR, HD), BF16),
            pltpu.VMEM((HEADS, ZN, 2 * PAIR, HD), BF16),
            pltpu.VMEM((HEADS, ZN, NL, 2 * PAIR), F32),
            pltpu.VMEM((HEADS, ZN, NL, 2 * PAIR), F32),
            pltpu.VMEM((HEADS, DP * 2, PAIR), F32),
            pltpu.VMEM((HEADS, DP, DP * 2, PAIR), F32),
            pltpu.VMEM((HEADS, DP, PAIR, HD), BF16),
            pltpu.VMEM((HEADS, DP, PAIR, HD), BF16),
            pltpu.VMEM((HEADS, ROWS, 2 * HD), BF16),
            pltpu.VMEM((HEADS, ZN, SHARD, 2 * HD), BF16),
            pltpu.VMEM((HEADS, ZN, SHARD, 2 * HD), BF16),
            pltpu.VMEM((HEADS, 2, 4, SHARD, 2 * HD), BF16),
            pltpu.VMEM((HEADS, 2, 4, SHARD, 2 * HD), BF16),
            pltpu.VMEM((2, 2, SIDE, CHUNK, SHARD), BF16),
            pltpu.VMEM((2, 2, SIDE, CHUNK, SHARD), BF16),
            pltpu.VMEM((2, 2, SIDE, HALF, SHARD), BF16),
            pltpu.VMEM((2, 2, SIDE, HALF, SHARD), BF16),
            pltpu.VMEM((2, SIDE, HALF, SHARD), F32),
            pltpu.VMEM((2, 2, CHUNK, SHARD), BF16),
            pltpu.VMEM((2, 2, CHUNK, SHARD), BF16),
            pltpu.VMEM((2, 2, HALF, SHARD), BF16),
            pltpu.VMEM((2, 2, HALF, SHARD), BF16),
            dma((3,)), dma((22,)),
            dma((HEADS, 2, 2, 4)), dma((HEADS, 3)),
            dma((2, 4)), dma((1,)),
            dma((2, 2)), dma((2,)), dma((2, 4, 2)), dma((1,)),
            dma((HEADS, ZN)), dma((HEADS,)), dma((HEADS,)),
            dma((HEADS, 5)), dma((HEADS, 2, 4)),
            dma((2, 2)), dma((2,)), dma((2, 2)), dma((2,)),
        ],
        compiler_params=pltpu.CompilerParams(
            collective_id=0, has_side_effects=True, vmem_limit_bytes=60 * 2**20
        ),
        name="retro_backward",
    )(ids, queries, grad_attn, encoded, key_weight, value_weight)
    return pl.pallas_call(
        publish_kernel,
        out_shape=shapes,
        in_specs=[vmem] * 4,
        out_specs=(vmem,) * 4,
        name="publish",
    )(*results)


def solution(mesh):
    return jax.shard_map(
        body,
        mesh=mesh,
        in_specs=(
            P("dp", "mp"),
            P("dp", "mp"),
            P("dp", "mp"),
            P(None, "mp"),
            P(None, "mp"),
            P("dp", None),
        ),
        out_specs=(P("dp", "mp"), P("dp", "mp"), P("dp", "mp"), P("dp", "mp")),
        check_vma=False,
    )
```

```python
import math

import jax
import jax.numpy as jnp
from jax import lax
from jax.experimental import pallas as pl
from jax.experimental.pallas import tpu as pltpu
from jax.sharding import PartitionSpec as P

HD = 128
SPAN = 64
NL = 128
K = 2
NB_DEV = 4
HEADS = 2
DP = 16
MP = 16
ZN = 8
SIDE = 4
SHARD = 256
ROWS = 512
HALF = 256
CHUNK = 128
PAIR = 2 * SPAN
MESH = pl.DeviceIdType.MESH
SCALE = 1.0 / math.sqrt(HD)
OFFSETS = (0, -1, 1, 2)
SPAN_MASK = 7
RING = (4, 3, -3, 2, -2, 1, -1, 0)
NT = (((1,), (1,)), ((), ()))
NN = (((1,), (0,)), ((), ()))
TN = (((0,), (0,)), ((), ()))
BF16, F32, I32 = jnp.bfloat16, jnp.float32, jnp.int32


def dot(a, b, dims):
    return lax.dot_general(a, b, dims, preferred_element_type=F32)


def wrap(value, size):
    return lax.rem(value + size, size)


class Place:
    def __init__(self):
        self.dp = lax.axis_index("dp")
        self.mp = lax.axis_index("mp")
        self.z, self.core = lax.div(self.dp, 2), lax.rem(self.dp, 2)
        self.x, self.y = lax.div(self.mp, SIDE), lax.rem(self.mp, SIDE)
        self.sibling = self.z * 2 + 1 - self.core

    def along_z(self, step, other_core=False):
        core = 1 - self.core if other_core else self.core
        return wrap(self.z + step, ZN) * 2 + core

    def in_plane(self, path, first, second):
        along_x, along_y = (first, second) if path == 0 else (second, first)
        return wrap(self.x + along_x, SIDE) * SIDE + wrap(self.y + along_y, SIDE)

    def plane_neighbour(self, path, axis, way):
        step = 1 if way == 0 else -1
        return self.in_plane(path, step, 0) if axis == 0 else self.in_plane(path, 0, step)

    def z_device(self, way):
        return (self.along_z(1 if way == 0 else -1), self.mp)

    def greet(self):
        barrier = pltpu.get_barrier_semaphore()
        others = [(wrap(self.dp + k, DP), self.mp) for k in range(1, DP)]
        others += [(self.dp, self.plane_neighbour(0, axis, way)) for axis in (0, 1) for way in (0, 1)]
        for device in others:
            pl.semaphore_signal(barrier, inc=1, device_id=device, device_id_type=MESH)
        pl.semaphore_wait(barrier, len(others))


def send(src, dst, send_sem, recv_sem, device):
    pltpu.make_async_remote_copy(
        src_ref=src,
        dst_ref=dst,
        send_sem=send_sem,
        recv_sem=recv_sem,
        device_id=device,
        device_id_type=MESH,
    ).start()


def landed(ref, sem):
    pltpu.make_async_copy(ref, ref, sem).wait()


def kernel(
    ids_ref, q_ref, g_ref, e_ref, kw_ref, vw_ref,
    dq_out, eg_out, kg_out, vg_out,
    q_all, g_all, ids_all, tab, enc, w, kacc, acc, kv, kt, q_sel, g_sel, score_sv, pgrad_sv, st_own, st_all,
    dqs, dqr, bg, csb, crb, zsb, zrb, xs1, xr1, near, xs2, xr2, group, ys1, yr1, ys2, yr2,
    local_sem, sent, zr, cr, ir, icr, p1r, p1f, p2r, p2f, sr, scr, dqrs, wcr, wzr, x1r, x2r, y1r, y2r,
):
    at = Place()
    here = (at.sibling, at.mp)
    srcs, alls = (q_ref, g_ref), (q_all, g_all)
    own_cols = [slice(h * HD, (h + 1) * HD) for h in range(HEADS)]

    ids_all[at.dp] = ids_ref[...]
    at.greet()

    def z_send(way, step, kind, h):
        origin = at.along_z(1 - step if way == 0 else step - 1)
        dst = alls[kind].at[h, origin]
        src = srcs[kind].at[:, own_cols[h]] if step == 1 else dst
        send(src, dst, sent.at[h], zr.at[h, kind, way, step - 1], at.z_device(way))

    def core_send(which, kind, h, origin):
        dst = alls[kind].at[h, origin]
        src = srcs[kind].at[:, own_cols[h]] if which == 0 else dst
        distance = which if which < 5 else which - 4
        send(src, dst, sent.at[2 + h], cr.at[h, max(distance - 2, 0)], here)

    def carries(way, step, kind):
        return step < 4 or (step == 4 and way == kind)

    def z_arrive(step, h, kind):
        for way in (0, 1):
            if not carries(way, step, kind):
                continue
            origin = at.along_z(-step if way == 0 else step)
            landed(alls[kind].at[h, origin], zr.at[h, kind, way, step - 1])
            if carries(way, step + 1, kind):
                z_send(way, step + 1, kind, h)
            core_send(way * 4 + step, kind, h, origin)

    def z_start(h):
        for kind in (0, 1):
            for way in (0, 1):
                z_send(way, 1, kind, h)
        for kind in (0, 1):
            core_send(0, kind, h, at.dp)

    def core_arrived(h, near):
        landed(q_all.at[h, pl.ds(0, (10, 4, 2)[near])], cr.at[h, near])

    def ids_send(way, step):
        block = ids_all.at[at.along_z(1 - step if way == 0 else step - 1)]
        send(block, block, sent.at[4], ir.at[way, step - 1], at.z_device(way))

    def ids_core(origin):
        block = ids_all.at[origin]
        send(block, block, sent.at[5], icr.at[0], here)

    def ids_arrive(step):
        for way in (0, 1):
            if step == 4 and way == 1:
                continue
            origin = at.along_z(-step if way == 0 else step)
            landed(ids_all.at[origin], ir.at[way, step - 1])
            if step < 3 or (step == 3 and way == 0):
                ids_send(way, step + 1)
            ids_core(origin)

    def lane_sum(value):
        for hop in (64, 32, 16, 8, 4, 2, 1):
            value = value + pltpu.roll(value, hop, 1)
        return value

    def make_tables():
        landed(ids_all.at[pl.ds(0, ZN)], icr.at[0])
        ids = ids_all[:, 0, :]
        slot = lax.broadcasted_iota(I32, (DP, 128), 1)
        owners = jnp.right_shift(ids, 2)
        ranks = jnp.zeros((DP, 128), I32)
        for back in range(1, DP):
            same = (pltpu.roll(owners, back, 1) == owners) & (slot >= back)
            ranks = ranks + jnp.where(same, 1, 0)
        places = owners * 2 + ranks
        even = jnp.bitwise_and(slot, 1) == 0
        partner = jnp.where(even, pltpu.roll(places, 127, 1), pltpu.roll(places, 1, 1))
        code = jnp.right_shift(slot, 1) + 8 * jnp.bitwise_and(ids, 3) + 32 * partner + 1024
        for rank in (0, 1):
            mine = (owners == at.dp) & (ranks == rank) & (slot < DP)
            tab[rank] = lane_sum(jnp.where(mine, code, 0))
        tab[2] = jnp.where(slot < SPAN, tab[0], tab[1])
        tab[3] = places
        own = tab[3, pl.ds(at.dp, 1), :]
        diagonal = slot == lax.broadcasted_iota(I32, (DP, 128), 0)
        tab[3] = lane_sum(jnp.where(diagonal, own, 0))

    def rows_of(path):
        return pl.ds(path * HALF, HALF)

    def part_of(path, way):
        return pl.ds(path * HALF + way * CHUNK, CHUNK)

    def p2_first(path, k):
        origin = at.in_plane(path, OFFSETS[k], 0)
        dst = enc.at[origin, rows_of(path)]
        src = e_ref.at[rows_of(path)] if k == 0 else dst
        for way in (0, 1):
            device = (at.dp, at.plane_neighbour(path, 1, way))
            send(src, dst, sent.at[7], p2r.at[path, k, way], device)

    def p1_first(path):
        for way in (0, 1):
            device = (at.dp, at.plane_neighbour(path, 0, way))
            send(
                e_ref.at[rows_of(path)], enc.at[at.mp, rows_of(path)],
                sent.at[6], p1r.at[path, way], device,
            )

    def p1_arrive(path, way):
        origin = at.in_plane(path, -1 if way == 0 else 1, 0)
        landed(enc.at[origin, rows_of(path)], p1r.at[path, way])
        part = enc.at[origin, part_of(path, way)]
        device = (at.dp, at.plane_neighbour(path, 0, way))
        send(part, part, sent.at[6], p1f.at[path], device)
        p2_first(path, 1 + way)

    def p1_far(path):
        landed(enc.at[at.in_plane(path, 2, 0), rows_of(path)], p1f.at[path])
        p2_first(path, 3)

    def p2_arrive(path, k):
        for way in (0, 1):
            origin = at.in_plane(path, OFFSETS[k], -1 if way == 0 else 1)
            landed(enc.at[origin, rows_of(path)], p2r.at[path, k, way])
            part = enc.at[origin, part_of(path, way)]
            device = (at.dp, at.plane_neighbour(path, 1, way))
            send(part, part, sent.at[7], p2f.at[0], device)

    def p2_far():
        landed(enc.at[pl.ds(0, SIDE)], p2f.at[0])

    def project_near(path, k):
        def one(h, carry):
            total = None
            for second in (0, -1, 1):
                origin = at.in_plane(path, OFFSETS[k], second)
                rows = pl.ds(pl.multiple_of(origin * SHARD, SHARD), SHARD)
                part = dot(enc[origin, rows_of(path), :], w[h, rows, :], NN)
                total = part if total is None else total + part
            if k == 0:
                kacc[h, rows_of(path), :] = total
            else:
                kacc[h, rows_of(path), :] += total
            return carry

        lax.fori_loop(0, HEADS, one, 0)

    def project_far():
        def one(h, carry):
            for path in (0, 1):
                total = kacc[h, rows_of(path), :]
                for k in range(SIDE):
                    origin = at.in_plane(path, OFFSETS[k], 2)
                    rows = pl.ds(pl.multiple_of(origin * SHARD, SHARD), SHARD)
                    total = total + dot(enc[origin, rows_of(path), :], w[h, rows, :], NN)
                kv[h, rows_of(path), :] = total.astype(BF16)
            kt[h] = jnp.transpose(kv[h, :, :HD])
            return carry

        lax.fori_loop(0, HEADS, one, 0)

    low = lax.broadcasted_iota(I32, (1, PAIR), 1) < SPAN

    def chosen(ref, h, i):
        picked = []
        for rank in (0, 1):
            span = jnp.bitwise_and(tab[rank, pl.ds(i, 1), :], SPAN_MASK)
            total = None
            for s in range(ROWS // SPAN):
                factor = jnp.where(span == s, 1.0, 0.0).astype(BF16)
                term = ref[h, i, pl.ds(s * SPAN, SPAN), :] * factor
                total = term if total is None else total + term
            picked.append(total)
        return jnp.concatenate(picked, axis=0)

    def lane_codes(chip):
        return jnp.concatenate([tab[2, pl.ds(chip * 2 + core, 1), :] for core in (0, 1)], axis=1)

    def blocks_of(codes):
        return jnp.bitwise_and(jnp.right_shift(codes, 3), 3)

    def chip_stats(h, chip):
        block = blocks_of(lane_codes(chip))
        qh, gh = q_sel[h, chip], g_sel[h, chip]
        scores = pgrad = None
        for b in range(NB_DEV):
            rows = pl.ds(b * NL, NL)
            s = dot(kv[h, rows, :HD], qh, NT)
            p = dot(kv[h, rows, HD:], gh, NT)
            scores = s if b == 0 else jnp.where(block == b, s, scores)
            pgrad = p if b == 0 else jnp.where(block == b, p, pgrad)
        scores = scores * SCALE
        top = jnp.max(scores, axis=0, keepdims=True)
        e = jnp.exp(scores - top)
        total = jnp.sum(e, axis=0, keepdims=True)
        lse = top + jnp.log(total)
        delta = jnp.sum(e * pgrad, axis=0, keepdims=True) / total
        for core in (0, 1):
            lanes = slice(core * PAIR, (core + 1) * PAIR)
            st_own[h, pl.ds(chip * 4 + core * 2, 1), :] = lse[:, lanes]
            st_own[h, pl.ds(chip * 4 + core * 2 + 1, 1), :] = delta[:, lanes]
        score_sv[h, chip] = scores
        pgrad_sv[h, chip] = pgrad

    def chips(h, distance, work):
        first, step, count = ((6, 1, 5), (3, 2, 2), (4, 1, 1))[distance]

        def one(t, carry):
            work(h, lax.rem(at.z + first + step * t, ZN))
            return carry

        lax.fori_loop(0, count, one, 0)

    def chip_select(h, chip):
        for ref, sel in ((q_all, q_sel), (g_all, g_sel)):
            for core in (0, 1):
                sel[h, chip, pl.ds(core * PAIR, PAIR), :] = chosen(ref, h, chip * 2 + core)

    def select(h, distance):
        core_arrived(h, distance)
        chips(h, distance, chip_select)

    def stats(h, distance):
        chips(h, distance, chip_stats)

    def stats_send(h):
        for k in (4, 3, 5, 2, 6, 1, 7):
            device = (at.along_z(k), at.mp)
            send(st_own.at[h], st_all.at[h, at.dp], sent.at[8 + h], sr.at[h, at.z], device)
        send(st_own.at[h], st_all.at[h, at.dp], sent.at[10 + h], scr.at[h], here)

    def stats_forward(h):
        for k in (1, 7, 2, 6, 3, 5, 4):
            origin = at.along_z(k)
            landed(st_all.at[h, origin], sr.at[h, wrap(at.z + k, ZN)])
            send(st_all.at[h, origin], st_all.at[h, origin], sent.at[10 + h], scr.at[h], here)

    def stats_arrived(h):
        landed(st_all.at[h, pl.ds(0, ZN)], scr.at[h])
        st_all[h, at.dp] = st_own[h]

    def merged(h, i):
        code = tab[2, pl.ds(i, 1), :]
        partner = jnp.bitwise_and(jnp.right_shift(code, 5), 31)
        owner = jnp.right_shift(partner, 1)
        turned = pltpu.roll(owner, SPAN, 1)
        straight = jnp.zeros((2, PAIR), F32)
        crossed = jnp.zeros((2, PAIR), F32)
        for o in range(DP):
            pair = st_all[h, o, pl.ds(i * 2, 2), :]
            straight = jnp.where(owner == o, pair, straight)
            crossed = jnp.where(turned == o, pair, crossed)
        same = (jnp.bitwise_and(partner, 1) == 0) == low
        there = jnp.where(same, straight, pltpu.roll(crossed, SPAN, 1))
        own = st_own[h, pl.ds(i * 2, 2), :]
        lse_here, lse_there = own[:1], there[:1]
        top = jnp.maximum(lse_here, lse_there)
        lse = top + jnp.log(jnp.exp(lse_here - top) + jnp.exp(lse_there - top))
        delta = jnp.exp(lse_here - lse) * own[1:] + jnp.exp(lse_there - lse) * there[1:]
        return lse, delta

    def chip_grads(h, chip):
        codes = lane_codes(chip)
        block = jnp.where(jnp.right_shift(codes, 10) > 0, blocks_of(codes), NB_DEV)
        parts = [merged(h, chip * 2 + core) for core in (0, 1)]
        lse = jnp.concatenate([p[0] for p in parts], axis=1)
        delta = jnp.concatenate([p[1] for p in parts], axis=1)
        prob = jnp.exp(score_sv[h, chip] - lse)
        score_grad = prob * (pgrad_sv[h, chip] - delta) * SCALE
        zero = jnp.zeros_like(prob)
        prob_by_block = jnp.concatenate(
            [jnp.where(block == b, prob, zero).astype(BF16) for b in range(NB_DEV)], axis=0
        )
        grad_by_block = jnp.concatenate(
            [jnp.where(block == b, score_grad, zero).astype(BF16) for b in range(NB_DEV)], axis=0
        )
        acc[:, :HD] += dot(grad_by_block, q_sel[h, chip], NN)
        acc[:, HD:] += dot(prob_by_block, g_sel[h, chip], NN)
        dq = jnp.transpose(dot(kt[h], grad_by_block, NN)).astype(BF16)
        for core in (0, 1):
            dqs[h, chip * 2 + core] = dq[core * PAIR : (core + 1) * PAIR, :]

    def grads_begin(h):
        acc[...] = jnp.zeros_like(acc)

    def grads_part(h, begin, end, sends):
        def one(t, carry):
            chip = lax.rem(at.z + 1 + t, ZN)
            chip_grads(h, chip)
            if sends:
                for core in (0, 1):
                    dq_copy(h, chip * 2 + core)
            return carry

        lax.fori_loop(begin, end, one, 0)

    def grads_end(h):
        chip_grads(h, at.z)
        dqr[h, at.dp] = dqs[h, at.dp]
        bg[h] = acc[...].astype(BF16)

    def dq_copy(h, i):
        send(dqs.at[h, i], dqr.at[h, at.dp], sent.at[12 + h], dqrs.at[h], (i, at.mp))

    def dq_send(h, offsets):
        for offset in offsets:
            for other_core in (False, True):
                if offset == 0 and not other_core:
                    continue
                i = at.along_z(offset, other_core)
                dq_copy(h, i)

    def dq_final(h):
        landed(dqr.at[h, pl.ds(0, DP - 1)], dqrs.at[h])

        def one(c, carry):
            places = [tab[3, pl.ds(c * K + k, 1), :] for k in range(K)]
            total = jnp.zeros((SPAN, HD), BF16)
            for m in range(2 * DP):
                hit = (places[0] == m) | (places[1] == m)
                factor = jnp.where(hit, 1.0, 0.0).astype(BF16)
                total = total + dqr[h, m // 2, pl.ds(m % 2 * SPAN, SPAN), :] * factor
            dq_out[pl.ds(pl.multiple_of(c * SPAN, SPAN), SPAN), own_cols[h]] = total
            return carry

        lax.fori_loop(0, ROWS // SPAN, one, 0)

    def weight_sibling(h, begin, end):
        def one(which, carry):
            near = lax.div(which + 1, 2)
            sign = 2 * lax.rem(which, 2) - 1
            target = wrap(at.z + sign * (4 - near), ZN)
            csb[h, target] = dot(enc[target * 2 + 1 - at.core], bg[h], TN).astype(BF16)
            send(csb.at[h, target], crb.at[h, target], sent.at[14 + h], wcr.at[h, near], here)
            return carry

        lax.fori_loop(begin, end, one, 0)

    def weight_met(h, near):
        landed(crb.at[h, pl.ds(0, 1 if near in (0, 4) else 2)], wcr.at[h, near])

    def weight_term(h, which):
        target = wrap(at.z + RING[which], ZN)
        return dot(enc[target * 2 + at.core], bg[h], TN) + crb[h, target].astype(F32)

    def z_region(step, way):
        return pl.ds(way * CHUNK, CHUNK) if step == 1 else pl.ds(0, SHARD)

    def weight_put(h, way, step, value):
        region = z_region(step, way)
        zsb[h, way, step - 1, region, :] = value.astype(BF16)
        send(
            zsb.at[h, way, step - 1, region], zrb.at[h, way, step - 1, region],
            sent.at[16 + h], wzr.at[h, way, step - 1], at.z_device(way),
        )

    def weight_step(h, step):
        if step == 1:
            weight_met(h, 0)
            value = weight_term(h, 0)
            for way in (0, 1):
                weight_put(h, way, 1, value[way * CHUNK : (way + 1) * CHUNK, :])
            return
        weight_met(h, step - 1)
        for way in (0, 1):
            which = 2 * step - 3 + way
            value = weight_term(h, which)
            region = z_region(step - 1, way)
            landed(zrb.at[h, way, step - 2, region], wzr.at[h, way, step - 2])
            came = zrb[h, way, step - 2, region, :].astype(F32)
            if step == 2:
                pieces = [value[:CHUNK, :], value[CHUNK:, :]]
                pieces[way] = pieces[way] + came
                value = jnp.concatenate(pieces, axis=0)
            else:
                value = value + came
            weight_put(h, way, step, value)

    def weight_final(h):
        weight_met(h, 4)
        value = weight_term(h, 7)
        for way in (0, 1):
            landed(zrb.at[h, way, 3], wzr.at[h, way, 3])
            value = value + zrb[h, way, 3].astype(F32)
        kg_out[:, own_cols[h]] = value[:, :HD]
        vg_out[:, own_cols[h]] = value[:, HD:]

    def width_part(path, offset, j):
        if path == 0:
            index = wrap(at.x + offset, SIDE) * SIDE + j
        else:
            index = j * SIDE + wrap(at.y + offset, SIDE)
        cols = pl.ds(pl.multiple_of(index * SHARD, SHARD), SHARD)
        return sum(dot(bg[h, rows_of(path), :], w[h, cols, :], NT) for h in range(HEADS))

    def width_far(path):
        def one(j, carry):
            value = width_part(path, 2, j).astype(BF16)
            for way in (0, 1):
                xs1[path, way, j] = value[way * CHUNK : (way + 1) * CHUNK, :]
            return carry

        lax.fori_loop(0, SIDE, one, 0)
        for way in (0, 1):
            device = (at.dp, at.plane_neighbour(path, 0, way))
            send(xs1.at[path, way], xr1.at[path, way], sent.at[18], x1r.at[path, way], device)

    def width_near(path):
        for way in (0, 1):
            def one(j, carry):
                value = width_part(path, 1 if way == 0 else -1, j)
                pieces = [value[:CHUNK, :], value[CHUNK:, :]]
                xs2[path, way, 1 - way, j] = pieces[1 - way].astype(BF16)
                near[path, way, j] = pieces[way]
                return carry

            lax.fori_loop(0, SIDE, one, 0)
            near_send(path, way, 1 - way)

    def near_send(path, way, part):
        device = (at.dp, at.plane_neighbour(path, 0, way))
        send(xs2.at[path, way, part], xr2.at[path, way, part], sent.at[19], x2r.at[path], device)

    def width_met(path, way):
        landed(xr1.at[path, way], x1r.at[path, way])
        for j in range(SIDE):
            xs2[path, way, way, j] = (near[path, way, j] + xr1[path, way, j].astype(F32)).astype(BF16)
        near_send(path, way, way)

    def second(path):
        return at.y if path == 0 else at.x

    def width_own(path):
        def one(j, carry):
            group[path, j] = width_part(path, 0, j)
            return carry

        lax.fori_loop(0, SIDE, one, 0)

    def second_send(path, way, part):
        device = (at.dp, at.plane_neighbour(path, 1, way))
        send(ys2.at[path, way, part], yr2.at[path, way, part], sent.at[21], y2r.at[path], device)

    def second_near(path, way):
        return wrap(second(path) + (1 if way == 0 else -1), SIDE)

    def width_turn(path):
        landed(xr2.at[path], x2r.at[path])

        def one(j, carry):
            for part in (0, 1):
                rows = pl.ds(part * CHUNK, CHUNK)
                came = xr2[path, 0, part, j].astype(F32) + xr2[path, 1, part, j].astype(F32)
                group[path, j, rows, :] += came
            return carry

        lax.fori_loop(0, SIDE, one, 0)
        far = wrap(second(path) + 2, SIDE)
        for way in (0, 1):
            ys1[path, way] = group[path, far, pl.ds(way * CHUNK, CHUNK), :].astype(BF16)
            device = (at.dp, at.plane_neighbour(path, 1, way))
            send(ys1.at[path, way], yr1.at[path, way], sent.at[20], y1r.at[path, way], device)
        for way in (0, 1):
            part = 1 - way
            piece = group[path, second_near(path, way), pl.ds(part * CHUNK, CHUNK), :]
            ys2[path, way, part] = piece.astype(BF16)
            second_send(path, way, part)

    def width_second(path):
        for way in (0, 1):
            landed(yr1.at[path, way], y1r.at[path, way])
            piece = group[path, second_near(path, way), pl.ds(way * CHUNK, CHUNK), :]
            ys2[path, way, way] = (piece + yr1[path, way].astype(F32)).astype(BF16)
            second_send(path, way, way)

    def width_final(path):
        landed(yr2.at[path], y2r.at[path])
        for part in (0, 1):
            value = group[path, second(path), pl.ds(part * CHUNK, CHUNK), :]
            for way in (0, 1):
                value = value + yr2[path, way, part].astype(F32)
            eg_out[pl.ds(path * HALF + part * CHUNK, CHUNK), :] = value.astype(BF16)

    def finish():
        for h in range(HEADS):
            landed(q_all.at[h, pl.ds(0, 14)], sent.at[h])
            landed(q_all.at[h], sent.at[2 + h])
            landed(st_all.at[h, pl.ds(0, ZN - 1)], sent.at[8 + h])
            landed(st_all.at[h, pl.ds(0, ZN)], sent.at[10 + h])
            landed(dqr.at[h, pl.ds(0, DP - 1)], sent.at[12 + h])
            landed(crb.at[h], sent.at[14 + h])
            landed(crb.at[h, pl.ds(0, 7)], sent.at[16 + h])
        landed(ids_all.at[pl.ds(0, 7)], sent.at[4])
        landed(ids_all.at[pl.ds(0, ZN)], sent.at[5])
        landed(enc.at[pl.ds(0, 3)], sent.at[6])
        landed(enc.at[pl.ds(0, 12)], sent.at[7])
        for n, ref in enumerate((xr1, xr2, yr1, yr2)):
            landed(ref, sent.at[18 + n])

    for way in (0, 1):
        ids_send(way, 1)
    z_start(0)
    ids_core(at.dp)
    for path in (0, 1):
        p1_first(path)
    for path in (0, 1):
        p2_first(path, 0)
    pltpu.make_async_copy(e_ref, enc.at[at.mp], local_sem.at[0]).start()
    for h in range(HEADS):
        cols = own_cols[h]
        pltpu.make_async_copy(q_ref.at[:, cols], q_all.at[h, at.dp], local_sem.at[1]).start()
        pltpu.make_async_copy(g_ref.at[:, cols], g_all.at[h, at.dp], local_sem.at[1]).start()
        pltpu.make_async_copy(kw_ref.at[:, cols], w.at[h, :, pl.ds(0, HD)], local_sem.at[2]).start()
        pltpu.make_async_copy(vw_ref.at[:, cols], w.at[h, :, pl.ds(HD, HD)], local_sem.at[2]).start()

    for way in (0, 1):
        for path in (0, 1):
            p1_arrive(path, way)
    z_arrive(1, 0, 0)
    z_arrive(1, 0, 1)
    z_start(1)
    for path in (0, 1):
        p2_arrive(path, 0)
    ids_arrive(1)
    for path in (0, 1):
        p1_far(path)
    z_arrive(2, 0, 0)
    landed(enc.at[0], local_sem.at[0])
    landed(q_all.at[0, pl.ds(0, 4)], local_sem.at[1])
    landed(w, local_sem.at[2])
    ids_arrive(2)
    z_arrive(2, 0, 1)
    for path in (0, 1):
        p2_arrive(path, 1)
    for path in (0, 1):
        project_near(path, 0)
    ids_arrive(3)
    z_arrive(3, 0, 0)
    for path in (0, 1):
        p2_arrive(path, 2)
    for path in (0, 1):
        project_near(path, 1)
    ids_arrive(4)
    z_arrive(3, 0, 1)
    for path in (0, 1):
        p2_arrive(path, 3)
    for path in (0, 1):
        project_near(path, 2)
    make_tables()
    z_arrive(1, 1, 0)
    select(0, 0)
    z_arrive(1, 1, 1)
    for path in (0, 1):
        project_near(path, 3)
    p2_far()
    project_far()
    stats(0, 0)
    z_arrive(4, 0, 0)
    z_arrive(4, 0, 1)
    z_arrive(2, 1, 0)
    select(0, 1)
    stats(0, 1)
    select(0, 2)
    stats(0, 2)
    stats_send(0)
    z_arrive(2, 1, 1)
    z_arrive(3, 1, 0)
    select(1, 0)
    stats_forward(0)
    z_arrive(3, 1, 1)
    stats(1, 0)
    stats_arrived(0)
    grads_begin(0)
    grads_part(0, 0, 4, True)
    z_arrive(4, 1, 0)
    z_arrive(4, 1, 1)
    grads_part(0, 4, 7, False)
    grads_end(0)
    weight_sibling(0, 0, 3)
    select(1, 1)
    stats(1, 1)
    select(1, 2)
    stats(1, 2)
    stats_send(1)
    weight_step(0, 1)
    dq_send(0, (5, 6))
    weight_sibling(0, 3, 8)
    stats_forward(1)
    dq_send(0, (7, 0))
    weight_step(0, 2)
    stats_arrived(1)
    grads_begin(1)
    grads_part(1, 0, 7, False)
    grads_end(1)
    for path in (0, 1):
        width_far(path)
    weight_sibling(1, 0, 3)
    weight_step(0, 3)
    weight_step(1, 1)
    dq_send(1, (1, 5))
    for path in (0, 1):
        width_near(path)
    weight_step(0, 4)
    weight_sibling(1, 3, 8)
    weight_step(1, 2)
    dq_send(1, (2, 6))
    for path in (0, 1):
        width_own(path)
    for way in (0, 1):
        for path in (0, 1):
            width_met(path, way)
    weight_step(1, 3)
    dq_send(1, (3, 7))
    weight_final(0)
    dq_final(0)
    weight_step(1, 4)
    dq_send(1, (4, 0))
    for path in (0, 1):
        width_turn(path)
    for path in (0, 1):
        width_second(path)
    for path in (0, 1):
        width_final(path)
    weight_final(1)
    dq_final(1)
    finish()


def publish_kernel(a, b, c, d, a_out, b_out, c_out, d_out):
    for src, dst in ((a, a_out), (b, b_out), (c, c_out), (d, d_out)):
        dst[...] = src[...]


def body(queries, grad_attn, encoded, key_weight, value_weight, nbr_ids):
    hbm = pl.BlockSpec(memory_space=pltpu.HBM)
    vmem = pl.BlockSpec(memory_space=pltpu.VMEM)
    dma = pltpu.SemaphoreType.DMA
    shapes = (
        jax.ShapeDtypeStruct((ROWS, SHARD), BF16),
        jax.ShapeDtypeStruct((ROWS, SHARD), BF16),
        jax.ShapeDtypeStruct((SHARD, SHARD), F32),
        jax.ShapeDtypeStruct((SHARD, SHARD), F32),
    )
    ids = jnp.pad(nbr_ids.reshape(1, DP), ((0, 7), (0, 128 - DP)))
    results = pl.pallas_call(
        kernel,
        out_shape=shapes,
        in_specs=[vmem] + [hbm] * 5,
        out_specs=(vmem, vmem, vmem, vmem),
        scratch_shapes=[
            pltpu.VMEM((HEADS, DP, ROWS, HD), BF16),
            pltpu.VMEM((HEADS, DP, ROWS, HD), BF16),
            pltpu.VMEM((DP, 8, 128), I32),
            pltpu.VMEM((4, DP, 128), I32),
            pltpu.VMEM((MP, ROWS, SHARD), BF16),
            pltpu.VMEM((HEADS, MP * SHARD, 2 * HD), BF16),
            pltpu.VMEM((HEADS, ROWS, 2 * HD), F32),
            pltpu.VMEM((ROWS, 2 * HD), F32),
            pltpu.VMEM((HEADS, ROWS, 2 * HD), BF16),
            pltpu.VMEM((HEADS, HD, ROWS), BF16),
            pltpu.VMEM((HEADS, ZN, 2 * PAIR, HD), BF16),
            pltpu.VMEM((HEADS, ZN, 2 * PAIR, HD), BF16),
            pltpu.VMEM((HEADS, ZN, NL, 2 * PAIR), F32),
            pltpu.VMEM((HEADS, ZN, NL, 2 * PAIR), F32),
            pltpu.VMEM((HEADS, DP * 2, PAIR), F32),
            pltpu.VMEM((HEADS, DP, DP * 2, PAIR), F32),
            pltpu.VMEM((HEADS, DP, PAIR, HD), BF16),
            pltpu.VMEM((HEADS, DP, PAIR, HD), BF16),
            pltpu.VMEM((HEADS, ROWS, 2 * HD), BF16),
            pltpu.VMEM((HEADS, ZN, SHARD, 2 * HD), BF16),
            pltpu.VMEM((HEADS, ZN, SHARD, 2 * HD), BF16),
            pltpu.VMEM((HEADS, 2, 4, SHARD, 2 * HD), BF16),
            pltpu.VMEM((HEADS, 2, 4, SHARD, 2 * HD), BF16),
            pltpu.VMEM((2, 2, SIDE, CHUNK, SHARD), BF16),
            pltpu.VMEM((2, 2, SIDE, CHUNK, SHARD), BF16),
            pltpu.VMEM((2, 2, SIDE, CHUNK, SHARD), F32),
            pltpu.VMEM((2, 2, 2, SIDE, CHUNK, SHARD), BF16),
            pltpu.VMEM((2, 2, 2, SIDE, CHUNK, SHARD), BF16),
            pltpu.VMEM((2, SIDE, HALF, SHARD), F32),
            pltpu.VMEM((2, 2, CHUNK, SHARD), BF16),
            pltpu.VMEM((2, 2, CHUNK, SHARD), BF16),
            pltpu.VMEM((2, 2, 2, CHUNK, SHARD), BF16),
            pltpu.VMEM((2, 2, 2, CHUNK, SHARD), BF16),
            dma((3,)), dma((22,)),
            dma((HEADS, 2, 2, 4)), dma((HEADS, 3)),
            dma((2, 4)), dma((1,)),
            dma((2, 2)), dma((2,)), dma((2, 4, 2)), dma((1,)),
            dma((HEADS, ZN)), dma((HEADS,)), dma((HEADS,)),
            dma((HEADS, 5)), dma((HEADS, 2, 4)),
            dma((2, 2)), dma((2,)), dma((2, 2)), dma((2,)),
        ],
        compiler_params=pltpu.CompilerParams(
            collective_id=0, has_side_effects=True, vmem_limit_bytes=60 * 2**20
        ),
        name="retro_backward",
    )(ids, queries, grad_attn, encoded, key_weight, value_weight)
    return pl.pallas_call(
        publish_kernel,
        out_shape=shapes,
        in_specs=[vmem] * 4,
        out_specs=(vmem,) * 4,
        name="publish",
    )(*results)


def solution(mesh):
    return jax.shard_map(
        body,
        mesh=mesh,
        in_specs=(
            P("dp", "mp"),
            P("dp", "mp"),
            P("dp", "mp"),
            P(None, "mp"),
            P(None, "mp"),
            P("dp", None),
        ),
        out_specs=(P("dp", "mp"), P("dp", "mp"), P("dp", "mp"), P("dp", "mp")),
        check_vma=False,
    )
```

```python
import math

import jax
import jax.numpy as jnp
from jax import lax
from jax.experimental import pallas as pl
from jax.experimental.pallas import tpu as pltpu
from jax.sharding import PartitionSpec as P

HD = 128
SPAN = 64
NL = 128
K = 2
NB_DEV = 4
HEADS = 2
DP = 16
MP = 16
ZN = 8
SIDE = 4
SHARD = 256
ROWS = 512
HALF = 256
CHUNK = 128
PAIR = 2 * SPAN
MESH = pl.DeviceIdType.MESH
SCALE = 1.0 / math.sqrt(HD)
OFFSETS = (0, -1, 1, 2)
SPAN_MASK = 7
RING = (4, 3, -3, 2, -2, 1, -1, 0)
NT = (((1,), (1,)), ((), ()))
NN = (((1,), (0,)), ((), ()))
TN = (((0,), (0,)), ((), ()))
BF16, F32, I32 = jnp.bfloat16, jnp.float32, jnp.int32


def dot(a, b, dims):
    return lax.dot_general(a, b, dims, preferred_element_type=F32)


def wrap(value, size):
    return lax.rem(value + size, size)


class Place:
    def __init__(self):
        self.dp = lax.axis_index("dp")
        self.mp = lax.axis_index("mp")
        self.z, self.core = lax.div(self.dp, 2), lax.rem(self.dp, 2)
        self.x, self.y = lax.div(self.mp, SIDE), lax.rem(self.mp, SIDE)
        self.sibling = self.z * 2 + 1 - self.core

    def along_z(self, step, other_core=False):
        core = 1 - self.core if other_core else self.core
        return wrap(self.z + step, ZN) * 2 + core

    def in_plane(self, path, first, second):
        along_x, along_y = (first, second) if path == 0 else (second, first)
        return wrap(self.x + along_x, SIDE) * SIDE + wrap(self.y + along_y, SIDE)

    def plane_neighbour(self, path, axis, way):
        step = 1 if way == 0 else -1
        return self.in_plane(path, step, 0) if axis == 0 else self.in_plane(path, 0, step)

    def z_device(self, way):
        return (self.along_z(1 if way == 0 else -1), self.mp)

    def greet(self):
        barrier = pltpu.get_barrier_semaphore()
        others = [self.z_device(0), self.z_device(1), (self.sibling, self.mp)]
        others += [(self.dp, self.plane_neighbour(0, axis, way)) for axis in (0, 1) for way in (0, 1)]
        for device in others:
            pl.semaphore_signal(barrier, inc=1, device_id=device, device_id_type=MESH)
        pl.semaphore_wait(barrier, len(others))


def send(src, dst, send_sem, recv_sem, device):
    pltpu.make_async_remote_copy(
        src_ref=src,
        dst_ref=dst,
        send_sem=send_sem,
        recv_sem=recv_sem,
        device_id=device,
        device_id_type=MESH,
    ).start()


def landed(ref, sem):
    pltpu.make_async_copy(ref, ref, sem).wait()


def kernel(
    ids_ref, q_ref, g_ref, e_ref, kw_ref, vw_ref,
    dq_out, eg_out, kg_out, vg_out,
    q_all, g_all, ids_all, tab, enc, w, kacc, acc, kv, kt, q_sel, g_sel, score_sv, pgrad_sv, st_own, st_all,
    dqs, dqr, bg, csb, crb, zsb, zrb, xs1, xr1, near, xs2, xr2, group, ys1, yr1, ys2, yr2,
    local_sem, sent, zr, cr, ir, icr, p1r, p1f, p2r, p2f, sr, scr, dqrs, wcr, wzr, x1r, x2r, y1r, y2r,
):
    at = Place()
    here = (at.sibling, at.mp)
    srcs, alls = (q_ref, g_ref), (q_all, g_all)
    own_cols = [slice(h * HD, (h + 1) * HD) for h in range(HEADS)]

    ids_all[at.dp] = ids_ref[...]
    at.greet()

    def z_send(way, step, kind, h):
        origin = at.along_z(1 - step if way == 0 else step - 1)
        dst = alls[kind].at[h, origin]
        src = srcs[kind].at[:, own_cols[h]] if step == 1 else dst
        send(src, dst, sent.at[h], zr.at[h, kind, way, step - 1], at.z_device(way))

    def core_send(which, kind, h, origin):
        dst = alls[kind].at[h, origin]
        src = srcs[kind].at[:, own_cols[h]] if which == 0 else dst
        distance = which if which < 5 else which - 4
        send(src, dst, sent.at[2 + h], cr.at[h, max(distance - 2, 0)], here)

    def carries(way, step, kind):
        return step < 4 or (step == 4 and way == kind)

    def z_arrive(step, h, kind):
        for way in (0, 1):
            if not carries(way, step, kind):
                continue
            origin = at.along_z(-step if way == 0 else step)
            landed(alls[kind].at[h, origin], zr.at[h, kind, way, step - 1])
            if carries(way, step + 1, kind):
                z_send(way, step + 1, kind, h)
            core_send(way * 4 + step, kind, h, origin)

    def z_start(h):
        for kind in (0, 1):
            for way in (0, 1):
                z_send(way, 1, kind, h)
        for kind in (0, 1):
            core_send(0, kind, h, at.dp)

    def core_arrived(h, near):
        landed(q_all.at[h, pl.ds(0, (10, 4, 2)[near])], cr.at[h, near])

    def ids_send(way, step):
        block = ids_all.at[at.along_z(1 - step if way == 0 else step - 1)]
        send(block, block, sent.at[4], ir.at[way, step - 1], at.z_device(way))

    def ids_core(origin):
        block = ids_all.at[origin]
        send(block, block, sent.at[5], icr.at[0], here)

    def ids_arrive(step):
        for way in (0, 1):
            if step == 4 and way == 1:
                continue
            origin = at.along_z(-step if way == 0 else step)
            landed(ids_all.at[origin], ir.at[way, step - 1])
            if step < 3 or (step == 3 and way == 0):
                ids_send(way, step + 1)
            ids_core(origin)

    def lane_sum(value):
        for hop in (64, 32, 16, 8, 4, 2, 1):
            value = value + pltpu.roll(value, hop, 1)
        return value

    def make_tables():
        landed(ids_all.at[pl.ds(0, ZN)], icr.at[0])
        ids = ids_all[:, 0, :]
        slot = lax.broadcasted_iota(I32, (DP, 128), 1)
        owners = jnp.right_shift(ids, 2)
        ranks = jnp.zeros((DP, 128), I32)
        for back in range(1, DP):
            same = (pltpu.roll(owners, back, 1) == owners) & (slot >= back)
            ranks = ranks + jnp.where(same, 1, 0)
        places = owners * 2 + ranks
        even = jnp.bitwise_and(slot, 1) == 0
        partner = jnp.where(even, pltpu.roll(places, 127, 1), pltpu.roll(places, 1, 1))
        code = jnp.right_shift(slot, 1) + 8 * jnp.bitwise_and(ids, 3) + 32 * partner + 1024
        for rank in (0, 1):
            mine = (owners == at.dp) & (ranks == rank) & (slot < DP)
            tab[rank] = lane_sum(jnp.where(mine, code, 0))
        tab[2] = jnp.where(slot < SPAN, tab[0], tab[1])
        tab[3] = places
        own = tab[3, pl.ds(at.dp, 1), :]
        diagonal = slot == lax.broadcasted_iota(I32, (DP, 128), 0)
        tab[3] = lane_sum(jnp.where(diagonal, own, 0))

    def rows_of(path):
        return pl.ds(path * HALF, HALF)

    def part_of(path, way):
        return pl.ds(path * HALF + way * CHUNK, CHUNK)

    def p2_first(path, k):
        origin = at.in_plane(path, OFFSETS[k], 0)
        dst = enc.at[origin, rows_of(path)]
        src = e_ref.at[rows_of(path)] if k == 0 else dst
        for way in (0, 1):
            device = (at.dp, at.plane_neighbour(path, 1, way))
            send(src, dst, sent.at[7], p2r.at[path, k, way], device)

    def p1_first(path):
        for way in (0, 1):
            device = (at.dp, at.plane_neighbour(path, 0, way))
            send(
                e_ref.at[rows_of(path)], enc.at[at.mp, rows_of(path)],
                sent.at[6], p1r.at[path, way], device,
            )

    def p1_arrive(path, way):
        origin = at.in_plane(path, -1 if way == 0 else 1, 0)
        landed(enc.at[origin, rows_of(path)], p1r.at[path, way])
        part = enc.at[origin, part_of(path, way)]
        device = (at.dp, at.plane_neighbour(path, 0, way))
        send(part, part, sent.at[6], p1f.at[path], device)
        p2_first(path, 1 + way)

    def p1_far(path):
        landed(enc.at[at.in_plane(path, 2, 0), rows_of(path)], p1f.at[path])
        p2_first(path, 3)

    def p2_arrive(path, k):
        for way in (0, 1):
            origin = at.in_plane(path, OFFSETS[k], -1 if way == 0 else 1)
            landed(enc.at[origin, rows_of(path)], p2r.at[path, k, way])
            part = enc.at[origin, part_of(path, way)]
            device = (at.dp, at.plane_neighbour(path, 1, way))
            send(part, part, sent.at[7], p2f.at[0], device)

    def p2_far():
        landed(enc.at[pl.ds(0, SIDE)], p2f.at[0])

    def project_near(path, k):
        def one(h, carry):
            total = None
            for second in (0, -1, 1):
                origin = at.in_plane(path, OFFSETS[k], second)
                rows = pl.ds(pl.multiple_of(origin * SHARD, SHARD), SHARD)
                part = dot(enc[origin, rows_of(path), :], w[h, rows, :], NN)
                total = part if total is None else total + part
            if k == 0:
                kacc[h, rows_of(path), :] = total
            else:
                kacc[h, rows_of(path), :] += total
            return carry

        lax.fori_loop(0, HEADS, one, 0)

    def project_far():
        def one(h, carry):
            for path in (0, 1):
                total = kacc[h, rows_of(path), :]
                for k in range(SIDE):
                    origin = at.in_plane(path, OFFSETS[k], 2)
                    rows = pl.ds(pl.multiple_of(origin * SHARD, SHARD), SHARD)
                    total = total + dot(enc[origin, rows_of(path), :], w[h, rows, :], NN)
                kv[h, rows_of(path), :] = total.astype(BF16)
            kt[h] = jnp.transpose(kv[h, :, :HD])
            return carry

        lax.fori_loop(0, HEADS, one, 0)

    low = lax.broadcasted_iota(I32, (1, PAIR), 1) < SPAN

    def chosen(ref, h, i):
        picked = []
        for rank in (0, 1):
            span = jnp.bitwise_and(tab[rank, pl.ds(i, 1), :], SPAN_MASK)
            total = None
            for s in range(ROWS // SPAN):
                factor = jnp.where(span == s, 1.0, 0.0).astype(BF16)
                term = ref[h, i, pl.ds(s * SPAN, SPAN), :] * factor
                total = term if total is None else total + term
            picked.append(total)
        return jnp.concatenate(picked, axis=0)

    def lane_codes(chip):
        return jnp.concatenate([tab[2, pl.ds(chip * 2 + core, 1), :] for core in (0, 1)], axis=1)

    def blocks_of(codes):
        return jnp.bitwise_and(jnp.right_shift(codes, 3), 3)

    def chip_stats(h, chip):
        block = blocks_of(lane_codes(chip))
        qh, gh = q_sel[h, chip], g_sel[h, chip]
        scores = pgrad = None
        for b in range(NB_DEV):
            rows = pl.ds(b * NL, NL)
            s = dot(kv[h, rows, :HD], qh, NT)
            p = dot(kv[h, rows, HD:], gh, NT)
            scores = s if b == 0 else jnp.where(block == b, s, scores)
            pgrad = p if b == 0 else jnp.where(block == b, p, pgrad)
        scores = scores * SCALE
        top = jnp.max(scores, axis=0, keepdims=True)
        e = jnp.exp(scores - top)
        total = jnp.sum(e, axis=0, keepdims=True)
        lse = top + jnp.log(total)
        delta = jnp.sum(e * pgrad, axis=0, keepdims=True) / total
        for core in (0, 1):
            lanes = slice(core * PAIR, (core + 1) * PAIR)
            st_own[h, pl.ds(chip * 4 + core * 2, 1), :] = lse[:, lanes]
            st_own[h, pl.ds(chip * 4 + core * 2 + 1, 1), :] = delta[:, lanes]
        score_sv[h, chip] = scores
        pgrad_sv[h, chip] = pgrad

    def chips(h, distance, work):
        first, step, count = ((6, 1, 5), (3, 2, 2), (4, 1, 1))[distance]

        def one(t, carry):
            work(h, lax.rem(at.z + first + step * t, ZN))
            return carry

        lax.fori_loop(0, count, one, 0)

    def chip_select(h, chip):
        for ref, sel in ((q_all, q_sel), (g_all, g_sel)):
            for core in (0, 1):
                sel[h, chip, pl.ds(core * PAIR, PAIR), :] = chosen(ref, h, chip * 2 + core)

    def select(h, distance):
        core_arrived(h, distance)
        chips(h, distance, chip_select)

    def stats(h, distance):
        chips(h, distance, chip_stats)

    def stats_send(h):
        for k in (4, 3, 5, 2, 6, 1, 7):
            device = (at.along_z(k), at.mp)
            send(st_own.at[h], st_all.at[h, at.dp], sent.at[8 + h], sr.at[h, at.z], device)
        send(st_own.at[h], st_all.at[h, at.dp], sent.at[10 + h], scr.at[h], here)

    def stats_forward(h):
        for k in (1, 7, 2, 6, 3, 5, 4):
            origin = at.along_z(k)
            landed(st_all.at[h, origin], sr.at[h, wrap(at.z + k, ZN)])
            send(st_all.at[h, origin], st_all.at[h, origin], sent.at[10 + h], scr.at[h], here)

    def stats_arrived(h):
        landed(st_all.at[h, pl.ds(0, ZN)], scr.at[h])
        st_all[h, at.dp] = st_own[h]

    def merged(h, i):
        code = tab[2, pl.ds(i, 1), :]
        partner = jnp.bitwise_and(jnp.right_shift(code, 5), 31)
        owner = jnp.right_shift(partner, 1)
        turned = pltpu.roll(owner, SPAN, 1)
        straight = jnp.zeros((2, PAIR), F32)
        crossed = jnp.zeros((2, PAIR), F32)
        for o in range(DP):
            pair = st_all[h, o, pl.ds(i * 2, 2), :]
            straight = jnp.where(owner == o, pair, straight)
            crossed = jnp.where(turned == o, pair, crossed)
        same = (jnp.bitwise_and(partner, 1) == 0) == low
        there = jnp.where(same, straight, pltpu.roll(crossed, SPAN, 1))
        own = st_own[h, pl.ds(i * 2, 2), :]
        lse_here, lse_there = own[:1], there[:1]
        top = jnp.maximum(lse_here, lse_there)
        lse = top + jnp.log(jnp.exp(lse_here - top) + jnp.exp(lse_there - top))
        delta = jnp.exp(lse_here - lse) * own[1:] + jnp.exp(lse_there - lse) * there[1:]
        return lse, delta

    def chip_grads(h, chip):
        codes = lane_codes(chip)
        block = jnp.where(jnp.right_shift(codes, 10) > 0, blocks_of(codes), NB_DEV)
        parts = [merged(h, chip * 2 + core) for core in (0, 1)]
        lse = jnp.concatenate([p[0] for p in parts], axis=1)
        delta = jnp.concatenate([p[1] for p in parts], axis=1)
        prob = jnp.exp(score_sv[h, chip] - lse)
        score_grad = prob * (pgrad_sv[h, chip] - delta) * SCALE
        zero = jnp.zeros_like(prob)
        prob_by_block = jnp.concatenate(
            [jnp.where(block == b, prob, zero).astype(BF16) for b in range(NB_DEV)], axis=0
        )
        grad_by_block = jnp.concatenate(
            [jnp.where(block == b, score_grad, zero).astype(BF16) for b in range(NB_DEV)], axis=0
        )
        acc[:, :HD] += dot(grad_by_block, q_sel[h, chip], NN)
        acc[:, HD:] += dot(prob_by_block, g_sel[h, chip], NN)
        dq = jnp.transpose(dot(kt[h], grad_by_block, NN)).astype(BF16)
        for core in (0, 1):
            dqs[h, chip * 2 + core] = dq[core * PAIR : (core + 1) * PAIR, :]

    def grads_begin(h):
        acc[...] = jnp.zeros_like(acc)

    def grads_part(h, begin, end, sends):
        def one(t, carry):
            chip = lax.rem(at.z + 1 + t, ZN)
            chip_grads(h, chip)
            if sends:
                for core in (0, 1):
                    dq_copy(h, chip * 2 + core)
            return carry

        lax.fori_loop(begin, end, one, 0)

    def grads_end(h):
        chip_grads(h, at.z)
        dqr[h, at.dp] = dqs[h, at.dp]
        bg[h] = acc[...].astype(BF16)

    def dq_copy(h, i):
        send(dqs.at[h, i], dqr.at[h, at.dp], sent.at[12 + h], dqrs.at[h], (i, at.mp))

    def dq_send(h, offsets):
        for offset in offsets:
            for other_core in (False, True):
                if offset == 0 and not other_core:
                    continue
                i = at.along_z(offset, other_core)
                dq_copy(h, i)

    def dq_final(h):
        landed(dqr.at[h, pl.ds(0, DP - 1)], dqrs.at[h])

        def one(c, carry):
            places = [tab[3, pl.ds(c * K + k, 1), :] for k in range(K)]
            total = jnp.zeros((SPAN, HD), BF16)
            for m in range(2 * DP):
                hit = (places[0] == m) | (places[1] == m)
                factor = jnp.where(hit, 1.0, 0.0).astype(BF16)
                total = total + dqr[h, m // 2, pl.ds(m % 2 * SPAN, SPAN), :] * factor
            dq_out[pl.ds(pl.multiple_of(c * SPAN, SPAN), SPAN), own_cols[h]] = total
            return carry

        lax.fori_loop(0, ROWS // SPAN, one, 0)

    def weight_sibling(h, begin, end):
        def one(which, carry):
            near = lax.div(which + 1, 2)
            sign = 2 * lax.rem(which, 2) - 1
            target = wrap(at.z + sign * (4 - near), ZN)
            csb[h, target] = dot(enc[target * 2 + 1 - at.core], bg[h], TN).astype(BF16)
            send(csb.at[h, target], crb.at[h, target], sent.at[14 + h], wcr.at[h, near], here)
            return carry

        lax.fori_loop(begin, end, one, 0)

    def weight_met(h, near):
        landed(crb.at[h, pl.ds(0, 1 if near in (0, 4) else 2)], wcr.at[h, near])

    def weight_term(h, which):
        target = wrap(at.z + RING[which], ZN)
        return dot(enc[target * 2 + at.core], bg[h], TN) + crb[h, target].astype(F32)

    def z_region(step, way):
        return pl.ds(way * CHUNK, CHUNK) if step == 1 else pl.ds(0, SHARD)

    def weight_put(h, way, step, value):
        region = z_region(step, way)
        zsb[h, way, step - 1, region, :] = value.astype(BF16)
        send(
            zsb.at[h, way, step - 1, region], zrb.at[h, way, step - 1, region],
            sent.at[16 + h], wzr.at[h, way, step - 1], at.z_device(way),
        )

    def weight_step(h, step):
        if step == 1:
            weight_met(h, 0)
            value = weight_term(h, 0)
            for way in (0, 1):
                weight_put(h, way, 1, value[way * CHUNK : (way + 1) * CHUNK, :])
            return
        weight_met(h, step - 1)
        for way in (0, 1):
            which = 2 * step - 3 + way
            value = weight_term(h, which)
            region = z_region(step - 1, way)
            landed(zrb.at[h, way, step - 2, region], wzr.at[h, way, step - 2])
            came = zrb[h, way, step - 2, region, :].astype(F32)
            if step == 2:
                pieces = [value[:CHUNK, :], value[CHUNK:, :]]
                pieces[way] = pieces[way] + came
                value = jnp.concatenate(pieces, axis=0)
            else:
                value = value + came
            weight_put(h, way, step, value)

    def weight_final(h):
        weight_met(h, 4)
        value = weight_term(h, 7)
        for way in (0, 1):
            landed(zrb.at[h, way, 3], wzr.at[h, way, 3])
            value = value + zrb[h, way, 3].astype(F32)
        kg_out[:, own_cols[h]] = value[:, :HD]
        vg_out[:, own_cols[h]] = value[:, HD:]

    def width_part(path, offset, j):
        if path == 0:
            index = wrap(at.x + offset, SIDE) * SIDE + j
        else:
            index = j * SIDE + wrap(at.y + offset, SIDE)
        cols = pl.ds(pl.multiple_of(index * SHARD, SHARD), SHARD)
        return sum(dot(bg[h, rows_of(path), :], w[h, cols, :], NT) for h in range(HEADS))

    def width_far(path):
        def one(j, carry):
            value = width_part(path, 2, j).astype(BF16)
            for way in (0, 1):
                xs1[path, way, j] = value[way * CHUNK : (way + 1) * CHUNK, :]
            return carry

        lax.fori_loop(0, SIDE, one, 0)
        for way in (0, 1):
            device = (at.dp, at.plane_neighbour(path, 0, way))
            send(xs1.at[path, way], xr1.at[path, way], sent.at[18], x1r.at[path, way], device)

    def width_near(path):
        for way in (0, 1):
            def one(j, carry):
                value = width_part(path, 1 if way == 0 else -1, j)
                pieces = [value[:CHUNK, :], value[CHUNK:, :]]
                xs2[path, way, 1 - way, j] = pieces[1 - way].astype(BF16)
                near[path, way, j] = pieces[way]
                return carry

            lax.fori_loop(0, SIDE, one, 0)
            near_send(path, way, 1 - way)

    def near_send(path, way, part):
        device = (at.dp, at.plane_neighbour(path, 0, way))
        send(xs2.at[path, way, part], xr2.at[path, way, part], sent.at[19], x2r.at[path], device)

    def width_met(path, way):
        landed(xr1.at[path, way], x1r.at[path, way])
        for j in range(SIDE):
            xs2[path, way, way, j] = (near[path, way, j] + xr1[path, way, j].astype(F32)).astype(BF16)
        near_send(path, way, way)

    def second(path):
        return at.y if path == 0 else at.x

    def width_own(path):
        def one(j, carry):
            group[path, j] = width_part(path, 0, j)
            return carry

        lax.fori_loop(0, SIDE, one, 0)

    def second_send(path, way, part):
        device = (at.dp, at.plane_neighbour(path, 1, way))
        send(ys2.at[path, way, part], yr2.at[path, way, part], sent.at[21], y2r.at[path], device)

    def second_near(path, way):
        return wrap(second(path) + (1 if way == 0 else -1), SIDE)

    def width_turn(path):
        landed(xr2.at[path], x2r.at[path])

        def one(j, carry):
            for part in (0, 1):
                rows = pl.ds(part * CHUNK, CHUNK)
                came = xr2[path, 0, part, j].astype(F32) + xr2[path, 1, part, j].astype(F32)
                group[path, j, rows, :] += came
            return carry

        lax.fori_loop(0, SIDE, one, 0)
        far = wrap(second(path) + 2, SIDE)
        for way in (0, 1):
            ys1[path, way] = group[path, far, pl.ds(way * CHUNK, CHUNK), :].astype(BF16)
            device = (at.dp, at.plane_neighbour(path, 1, way))
            send(ys1.at[path, way], yr1.at[path, way], sent.at[20], y1r.at[path, way], device)
        for way in (0, 1):
            part = 1 - way
            piece = group[path, second_near(path, way), pl.ds(part * CHUNK, CHUNK), :]
            ys2[path, way, part] = piece.astype(BF16)
            second_send(path, way, part)

    def width_second(path):
        for way in (0, 1):
            landed(yr1.at[path, way], y1r.at[path, way])
            piece = group[path, second_near(path, way), pl.ds(way * CHUNK, CHUNK), :]
            ys2[path, way, way] = (piece + yr1[path, way].astype(F32)).astype(BF16)
            second_send(path, way, way)

    def width_final(path):
        landed(yr2.at[path], y2r.at[path])
        for part in (0, 1):
            value = group[path, second(path), pl.ds(part * CHUNK, CHUNK), :]
            for way in (0, 1):
                value = value + yr2[path, way, part].astype(F32)
            eg_out[pl.ds(path * HALF + part * CHUNK, CHUNK), :] = value.astype(BF16)

    def finish():
        for h in range(HEADS):
            landed(q_all.at[h, pl.ds(0, 14)], sent.at[h])
            landed(q_all.at[h], sent.at[2 + h])
            landed(st_all.at[h, pl.ds(0, ZN - 1)], sent.at[8 + h])
            landed(st_all.at[h, pl.ds(0, ZN)], sent.at[10 + h])
            landed(dqr.at[h, pl.ds(0, DP - 1)], sent.at[12 + h])
            landed(crb.at[h], sent.at[14 + h])
            landed(crb.at[h, pl.ds(0, 7)], sent.at[16 + h])
        landed(ids_all.at[pl.ds(0, 7)], sent.at[4])
        landed(ids_all.at[pl.ds(0, ZN)], sent.at[5])
        landed(enc.at[pl.ds(0, 3)], sent.at[6])
        landed(enc.at[pl.ds(0, 12)], sent.at[7])
        for n, ref in enumerate((xr1, xr2, yr1, yr2)):
            landed(ref, sent.at[18 + n])

    for way in (0, 1):
        ids_send(way, 1)
    z_start(0)
    ids_core(at.dp)
    for path in (0, 1):
        p1_first(path)
    for path in (0, 1):
        p2_first(path, 0)
    pltpu.make_async_copy(e_ref, enc.at[at.mp], local_sem.at[0]).start()
    for h in range(HEADS):
        cols = own_cols[h]
        pltpu.make_async_copy(q_ref.at[:, cols], q_all.at[h, at.dp], local_sem.at[1]).start()
        pltpu.make_async_copy(g_ref.at[:, cols], g_all.at[h, at.dp], local_sem.at[1]).start()
        pltpu.make_async_copy(kw_ref.at[:, cols], w.at[h, :, pl.ds(0, HD)], local_sem.at[2]).start()
        pltpu.make_async_copy(vw_ref.at[:, cols], w.at[h, :, pl.ds(HD, HD)], local_sem.at[2]).start()

    for way in (0, 1):
        for path in (0, 1):
            p1_arrive(path, way)
    z_arrive(1, 0, 0)
    z_arrive(1, 0, 1)
    z_start(1)
    for path in (0, 1):
        p2_arrive(path, 0)
    ids_arrive(1)
    for path in (0, 1):
        p1_far(path)
    z_arrive(2, 0, 0)
    landed(enc.at[0], local_sem.at[0])
    landed(q_all.at[0, pl.ds(0, 4)], local_sem.at[1])
    landed(w, local_sem.at[2])
    ids_arrive(2)
    z_arrive(2, 0, 1)
    for path in (0, 1):
        p2_arrive(path, 1)
    for path in (0, 1):
        project_near(path, 0)
    ids_arrive(3)
    z_arrive(3, 0, 0)
    for path in (0, 1):
        p2_arrive(path, 2)
    for path in (0, 1):
        project_near(path, 1)
    ids_arrive(4)
    z_arrive(3, 0, 1)
    for path in (0, 1):
        p2_arrive(path, 3)
    for path in (0, 1):
        project_near(path, 2)
    make_tables()
    z_arrive(1, 1, 0)
    select(0, 0)
    z_arrive(1, 1, 1)
    for path in (0, 1):
        project_near(path, 3)
    p2_far()
    project_far()
    stats(0, 0)
    z_arrive(4, 0, 0)
    z_arrive(4, 0, 1)
    z_arrive(2, 1, 0)
    select(0, 1)
    stats(0, 1)
    select(0, 2)
    stats(0, 2)
    stats_send(0)
    z_arrive(2, 1, 1)
    z_arrive(3, 1, 0)
    select(1, 0)
    stats_forward(0)
    z_arrive(3, 1, 1)
    stats(1, 0)
    stats_arrived(0)
    grads_begin(0)
    grads_part(0, 0, 4, True)
    z_arrive(4, 1, 0)
    z_arrive(4, 1, 1)
    grads_part(0, 4, 7, False)
    grads_end(0)
    weight_sibling(0, 0, 3)
    select(1, 1)
    stats(1, 1)
    select(1, 2)
    stats(1, 2)
    stats_send(1)
    weight_step(0, 1)
    dq_send(0, (5, 6))
    weight_sibling(0, 3, 8)
    stats_forward(1)
    dq_send(0, (7, 0))
    weight_step(0, 2)
    stats_arrived(1)
    grads_begin(1)
    grads_part(1, 0, 7, False)
    grads_end(1)
    weight_sibling(1, 0, 3)
    width_far(0)
    width_far(1)
    weight_step(0, 3)
    weight_step(1, 1)
    dq_send(1, (4, 0))
    width_near(0)
    width_near(1)
    weight_step(0, 4)
    dq_send(1, (1, 5))
    weight_sibling(1, 3, 8)
    weight_step(1, 2)
    dq_send(1, (2, 6))
    width_own(0)
    width_own(1)
    for way in (0, 1):
        for path in (0, 1):
            width_met(path, way)
    weight_step(1, 3)
    dq_send(1, (3, 7))
    weight_final(0)
    dq_final(0)
    for path in (0, 1):
        width_turn(path)
    weight_step(1, 4)
    for path in (0, 1):
        width_second(path)
    dq_final(1)
    for path in (0, 1):
        width_final(path)
    weight_final(1)
    finish()


def publish_kernel(a, b, c, d, a_out, b_out, c_out, d_out):
    for src, dst in ((a, a_out), (b, b_out), (c, c_out), (d, d_out)):
        dst[...] = src[...]


def body(queries, grad_attn, encoded, key_weight, value_weight, nbr_ids):
    hbm = pl.BlockSpec(memory_space=pltpu.HBM)
    vmem = pl.BlockSpec(memory_space=pltpu.VMEM)
    dma = pltpu.SemaphoreType.DMA
    shapes = (
        jax.ShapeDtypeStruct((ROWS, SHARD), BF16),
        jax.ShapeDtypeStruct((ROWS, SHARD), BF16),
        jax.ShapeDtypeStruct((SHARD, SHARD), F32),
        jax.ShapeDtypeStruct((SHARD, SHARD), F32),
    )
    ids = jnp.pad(nbr_ids.reshape(1, DP), ((0, 7), (0, 128 - DP)))
    results = pl.pallas_call(
        kernel,
        out_shape=shapes,
        in_specs=[vmem] + [hbm] * 5,
        out_specs=(vmem, vmem, vmem, vmem),
        scratch_shapes=[
            pltpu.VMEM((HEADS, DP, ROWS, HD), BF16),
            pltpu.VMEM((HEADS, DP, ROWS, HD), BF16),
            pltpu.VMEM((DP, 8, 128), I32),
            pltpu.VMEM((4, DP, 128), I32),
            pltpu.VMEM((MP, ROWS, SHARD), BF16),
            pltpu.VMEM((HEADS, MP * SHARD, 2 * HD), BF16),
            pltpu.VMEM((HEADS, ROWS, 2 * HD), F32),
            pltpu.VMEM((ROWS, 2 * HD), F32),
            pltpu.VMEM((HEADS, ROWS, 2 * HD), BF16),
            pltpu.VMEM((HEADS, HD, ROWS), BF16),
            pltpu.VMEM((HEADS, ZN, 2 * PAIR, HD), BF16),
            pltpu.VMEM((HEADS, ZN, 2 * PAIR, HD), BF16),
            pltpu.VMEM((HEADS, ZN, NL, 2 * PAIR), F32),
            pltpu.VMEM((HEADS, ZN, NL, 2 * PAIR), F32),
            pltpu.VMEM((HEADS, DP * 2, PAIR), F32),
            pltpu.VMEM((HEADS, DP, DP * 2, PAIR), F32),
            pltpu.VMEM((HEADS, DP, PAIR, HD), BF16),
            pltpu.VMEM((HEADS, DP, PAIR, HD), BF16),
            pltpu.VMEM((HEADS, ROWS, 2 * HD), BF16),
            pltpu.VMEM((HEADS, ZN, SHARD, 2 * HD), BF16),
            pltpu.VMEM((HEADS, ZN, SHARD, 2 * HD), BF16),
            pltpu.VMEM((HEADS, 2, 4, SHARD, 2 * HD), BF16),
            pltpu.VMEM((HEADS, 2, 4, SHARD, 2 * HD), BF16),
            pltpu.VMEM((2, 2, SIDE, CHUNK, SHARD), BF16),
            pltpu.VMEM((2, 2, SIDE, CHUNK, SHARD), BF16),
            pltpu.VMEM((2, 2, SIDE, CHUNK, SHARD), F32),
            pltpu.VMEM((2, 2, 2, SIDE, CHUNK, SHARD), BF16),
            pltpu.VMEM((2, 2, 2, SIDE, CHUNK, SHARD), BF16),
            pltpu.VMEM((2, SIDE, HALF, SHARD), F32),
            pltpu.VMEM((2, 2, CHUNK, SHARD), BF16),
            pltpu.VMEM((2, 2, CHUNK, SHARD), BF16),
            pltpu.VMEM((2, 2, 2, CHUNK, SHARD), BF16),
            pltpu.VMEM((2, 2, 2, CHUNK, SHARD), BF16),
            dma((3,)), dma((22,)),
            dma((HEADS, 2, 2, 4)), dma((HEADS, 3)),
            dma((2, 4)), dma((1,)),
            dma((2, 2)), dma((2,)), dma((2, 4, 2)), dma((1,)),
            dma((HEADS, ZN)), dma((HEADS,)), dma((HEADS,)),
            dma((HEADS, 5)), dma((HEADS, 2, 4)),
            dma((2, 2)), dma((2,)), dma((2, 2)), dma((2,)),
        ],
        compiler_params=pltpu.CompilerParams(
            collective_id=0, has_side_effects=True, vmem_limit_bytes=60 * 2**20
        ),
        name="retro_backward",
    )(ids, queries, grad_attn, encoded, key_weight, value_weight)
    return pl.pallas_call(
        publish_kernel,
        out_shape=shapes,
        in_specs=[vmem] * 4,
        out_specs=(vmem,) * 4,
        name="publish",
    )(*results)


def solution(mesh):
    return jax.shard_map(
        body,
        mesh=mesh,
        in_specs=(
            P("dp", "mp"),
            P("dp", "mp"),
            P("dp", "mp"),
            P(None, "mp"),
            P(None, "mp"),
            P("dp", None),
        ),
        out_specs=(P("dp", "mp"), P("dp", "mp"), P("dp", "mp"), P("dp", "mp")),
        check_vma=False,
    )
```

```python
import math

import jax
import jax.numpy as jnp
from jax import lax
from jax.experimental import pallas as pl
from jax.experimental.pallas import tpu as pltpu
from jax.sharding import PartitionSpec as P

HD = 128
SPAN = 64
NL = 128
K = 2
NB_DEV = 4
HEADS = 2
DP = 16
MP = 16
ZN = 8
SIDE = 4
SHARD = 256
ROWS = 512
HALF = 256
CHUNK = 128
PAIR = 2 * SPAN
MESH = pl.DeviceIdType.MESH
SCALE = 1.0 / math.sqrt(HD)
OFFSETS = (0, -1, 1, 2)
SPAN_MASK = 7
RING = (4, 3, -3, 2, -2, 1, -1, 0)
NT = (((1,), (1,)), ((), ()))
NN = (((1,), (0,)), ((), ()))
TN = (((0,), (0,)), ((), ()))
BF16, F32, I32 = jnp.bfloat16, jnp.float32, jnp.int32


def dot(a, b, dims):
    return lax.dot_general(a, b, dims, preferred_element_type=F32)


def wrap(value, size):
    return lax.rem(value + size, size)


class Place:
    def __init__(self):
        self.dp = lax.axis_index("dp")
        self.mp = lax.axis_index("mp")
        self.z, self.core = lax.div(self.dp, 2), lax.rem(self.dp, 2)
        self.x, self.y = lax.div(self.mp, SIDE), lax.rem(self.mp, SIDE)
        self.sibling = self.z * 2 + 1 - self.core

    def along_z(self, step, other_core=False):
        core = 1 - self.core if other_core else self.core
        return wrap(self.z + step, ZN) * 2 + core

    def in_plane(self, path, first, second):
        along_x, along_y = (first, second) if path == 0 else (second, first)
        return wrap(self.x + along_x, SIDE) * SIDE + wrap(self.y + along_y, SIDE)

    def plane_neighbour(self, path, axis, way):
        step = 1 if way == 0 else -1
        return self.in_plane(path, step, 0) if axis == 0 else self.in_plane(path, 0, step)

    def z_device(self, way):
        return (self.along_z(1 if way == 0 else -1), self.mp)

    def greet(self):
        barrier = pltpu.get_barrier_semaphore()
        others = [self.z_device(0), self.z_device(1), (self.sibling, self.mp)]
        others += [(self.dp, self.plane_neighbour(0, axis, way)) for axis in (0, 1) for way in (0, 1)]
        for device in others:
            pl.semaphore_signal(barrier, inc=1, device_id=device, device_id_type=MESH)
        pl.semaphore_wait(barrier, len(others))


def send(src, dst, send_sem, recv_sem, device):
    pltpu.make_async_remote_copy(
        src_ref=src,
        dst_ref=dst,
        send_sem=send_sem,
        recv_sem=recv_sem,
        device_id=device,
        device_id_type=MESH,
    ).start()


def landed(ref, sem):
    pltpu.make_async_copy(ref, ref, sem).wait()


def kernel(
    ids_ref, q_ref, g_ref, e_ref, kw_ref, vw_ref,
    dq_out, eg_out, kg_out, vg_out,
    q_all, g_all, ids_all, tab, enc, w, kacc, acc, kv, kt, q_sel, g_sel, score_sv, pgrad_sv, st_own, st_all,
    dqs, dqr, bg, csb, crb, zsb, zrb, xs1, xr1, near, xs2, xr2, group, ys1, yr1, ys2, yr2,
    local_sem, sent, zr, cr, ir, icr, p1r, p1f, p2r, p2f, sr, scr, dqrs, wcr, wzr, x1r, x2r, y1r, y2r,
):
    at = Place()
    here = (at.sibling, at.mp)
    srcs, alls = (q_ref, g_ref), (q_all, g_all)
    own_cols = [slice(h * HD, (h + 1) * HD) for h in range(HEADS)]

    ids_all[at.dp] = ids_ref[...]
    at.greet()

    def z_send(way, step, kind, h):
        origin = at.along_z(1 - step if way == 0 else step - 1)
        dst = alls[kind].at[h, origin]
        src = srcs[kind].at[:, own_cols[h]] if step == 1 else dst
        send(src, dst, sent.at[h], zr.at[h, kind, way, step - 1], at.z_device(way))

    def core_send(which, kind, h, origin):
        dst = alls[kind].at[h, origin]
        src = srcs[kind].at[:, own_cols[h]] if which == 0 else dst
        distance = which if which < 5 else which - 4
        send(src, dst, sent.at[2 + h], cr.at[h, max(distance - 2, 0)], here)

    def carries(way, step, kind):
        return step < 4 or (step == 4 and way == kind)

    def z_arrive(step, h, kind):
        for way in (0, 1):
            if not carries(way, step, kind):
                continue
            origin = at.along_z(-step if way == 0 else step)
            landed(alls[kind].at[h, origin], zr.at[h, kind, way, step - 1])
            if carries(way, step + 1, kind):
                z_send(way, step + 1, kind, h)
            core_send(way * 4 + step, kind, h, origin)

    def z_start(h):
        for kind in (0, 1):
            for way in (0, 1):
                z_send(way, 1, kind, h)
        for kind in (0, 1):
            core_send(0, kind, h, at.dp)

    def core_arrived(h, near):
        landed(q_all.at[h, pl.ds(0, (10, 4, 2)[near])], cr.at[h, near])

    def ids_send(way, step):
        block = ids_all.at[at.along_z(1 - step if way == 0 else step - 1)]
        send(block, block, sent.at[4], ir.at[way, step - 1], at.z_device(way))

    def ids_core(origin):
        block = ids_all.at[origin]
        send(block, block, sent.at[5], icr.at[0], here)

    def ids_arrive(step):
        for way in (0, 1):
            if step == 4 and way == 1:
                continue
            origin = at.along_z(-step if way == 0 else step)
            landed(ids_all.at[origin], ir.at[way, step - 1])
            if step < 3 or (step == 3 and way == 0):
                ids_send(way, step + 1)
            ids_core(origin)

    def lane_sum(value):
        for hop in (64, 32, 16, 8, 4, 2, 1):
            value = value + pltpu.roll(value, hop, 1)
        return value

    def make_tables():
        landed(ids_all.at[pl.ds(0, ZN)], icr.at[0])
        ids = ids_all[:, 0, :]
        slot = lax.broadcasted_iota(I32, (DP, 128), 1)
        owners = jnp.right_shift(ids, 2)
        ranks = jnp.zeros((DP, 128), I32)
        for back in range(1, DP):
            same = (pltpu.roll(owners, back, 1) == owners) & (slot >= back)
            ranks = ranks + jnp.where(same, 1, 0)
        places = owners * 2 + ranks
        even = jnp.bitwise_and(slot, 1) == 0
        partner = jnp.where(even, pltpu.roll(places, 127, 1), pltpu.roll(places, 1, 1))
        code = jnp.right_shift(slot, 1) + 8 * jnp.bitwise_and(ids, 3) + 32 * partner + 1024
        for rank in (0, 1):
            mine = (owners == at.dp) & (ranks == rank) & (slot < DP)
            tab[rank] = lane_sum(jnp.where(mine, code, 0))
        tab[2] = jnp.where(slot < SPAN, tab[0], tab[1])
        tab[3] = places
        own = tab[3, pl.ds(at.dp, 1), :]
        diagonal = slot == lax.broadcasted_iota(I32, (DP, 128), 0)
        tab[3] = lane_sum(jnp.where(diagonal, own, 0))

    def rows_of(path):
        return pl.ds(path * HALF, HALF)

    def part_of(path, way):
        return pl.ds(path * HALF + way * CHUNK, CHUNK)

    def p2_first(path, k):
        origin = at.in_plane(path, OFFSETS[k], 0)
        dst = enc.at[origin, rows_of(path)]
        src = e_ref.at[rows_of(path)] if k == 0 else dst
        for way in (0, 1):
            device = (at.dp, at.plane_neighbour(path, 1, way))
            send(src, dst, sent.at[7], p2r.at[path, k, way], device)

    def p1_first(path):
        for way in (0, 1):
            device = (at.dp, at.plane_neighbour(path, 0, way))
            send(
                e_ref.at[rows_of(path)], enc.at[at.mp, rows_of(path)],
                sent.at[6], p1r.at[path, way], device,
            )

    def p1_arrive(path, way):
        origin = at.in_plane(path, -1 if way == 0 else 1, 0)
        landed(enc.at[origin, rows_of(path)], p1r.at[path, way])
        part = enc.at[origin, part_of(path, way)]
        device = (at.dp, at.plane_neighbour(path, 0, way))
        send(part, part, sent.at[6], p1f.at[path], device)
        p2_first(path, 1 + way)

    def p1_far(path):
        landed(enc.at[at.in_plane(path, 2, 0), rows_of(path)], p1f.at[path])
        p2_first(path, 3)

    def p2_arrive(path, k):
        for way in (0, 1):
            origin = at.in_plane(path, OFFSETS[k], -1 if way == 0 else 1)
            landed(enc.at[origin, rows_of(path)], p2r.at[path, k, way])
            part = enc.at[origin, part_of(path, way)]
            device = (at.dp, at.plane_neighbour(path, 1, way))
            send(part, part, sent.at[7], p2f.at[0], device)

    def p2_far():
        landed(enc.at[pl.ds(0, SIDE)], p2f.at[0])

    def project_near(path, k):
        def one(h, carry):
            total = None
            for second in (0, -1, 1):
                origin = at.in_plane(path, OFFSETS[k], second)
                rows = pl.ds(pl.multiple_of(origin * SHARD, SHARD), SHARD)
                part = dot(enc[origin, rows_of(path), :], w[h, rows, :], NN)
                total = part if total is None else total + part
            if k == 0:
                kacc[h, rows_of(path), :] = total
            else:
                kacc[h, rows_of(path), :] += total
            return carry

        lax.fori_loop(0, HEADS, one, 0)

    def project_far():
        def one(h, carry):
            for path in (0, 1):
                total = kacc[h, rows_of(path), :]
                for k in range(SIDE):
                    origin = at.in_plane(path, OFFSETS[k], 2)
                    rows = pl.ds(pl.multiple_of(origin * SHARD, SHARD), SHARD)
                    total = total + dot(enc[origin, rows_of(path), :], w[h, rows, :], NN)
                kv[h, rows_of(path), :] = total.astype(BF16)
            kt[h] = jnp.transpose(kv[h, :, :HD])
            return carry

        lax.fori_loop(0, HEADS, one, 0)

    low = lax.broadcasted_iota(I32, (1, PAIR), 1) < SPAN

    def chosen(ref, h, i):
        picked = []
        for rank in (0, 1):
            span = jnp.bitwise_and(tab[rank, pl.ds(i, 1), :], SPAN_MASK)
            total = None
            for s in range(ROWS // SPAN):
                factor = jnp.where(span == s, 1.0, 0.0).astype(BF16)
                term = ref[h, i, pl.ds(s * SPAN, SPAN), :] * factor
                total = term if total is None else total + term
            picked.append(total)
        return jnp.concatenate(picked, axis=0)

    def lane_codes(chip):
        return jnp.concatenate([tab[2, pl.ds(chip * 2 + core, 1), :] for core in (0, 1)], axis=1)

    def blocks_of(codes):
        return jnp.bitwise_and(jnp.right_shift(codes, 3), 3)

    def chip_stats(h, chip):
        block = blocks_of(lane_codes(chip))
        qh, gh = q_sel[h, chip], g_sel[h, chip]
        scores = pgrad = None
        for b in range(NB_DEV):
            rows = pl.ds(b * NL, NL)
            s = dot(kv[h, rows, :HD], qh, NT)
            p = dot(kv[h, rows, HD:], gh, NT)
            scores = s if b == 0 else jnp.where(block == b, s, scores)
            pgrad = p if b == 0 else jnp.where(block == b, p, pgrad)
        scores = scores * SCALE
        top = jnp.max(scores, axis=0, keepdims=True)
        e = jnp.exp(scores - top)
        total = jnp.sum(e, axis=0, keepdims=True)
        lse = top + jnp.log(total)
        delta = jnp.sum(e * pgrad, axis=0, keepdims=True) / total
        for core in (0, 1):
            lanes = slice(core * PAIR, (core + 1) * PAIR)
            st_own[h, pl.ds(chip * 4 + core * 2, 1), :] = lse[:, lanes]
            st_own[h, pl.ds(chip * 4 + core * 2 + 1, 1), :] = delta[:, lanes]
        score_sv[h, chip] = scores
        pgrad_sv[h, chip] = pgrad

    def chips(h, distance, work):
        first, step, count = ((6, 1, 5), (3, 2, 2), (4, 1, 1))[distance]

        def one(t, carry):
            work(h, lax.rem(at.z + first + step * t, ZN))
            return carry

        lax.fori_loop(0, count, one, 0)

    def chip_select(h, chip):
        for ref, sel in ((q_all, q_sel), (g_all, g_sel)):
            for core in (0, 1):
                sel[h, chip, pl.ds(core * PAIR, PAIR), :] = chosen(ref, h, chip * 2 + core)

    def select(h, distance):
        core_arrived(h, distance)
        chips(h, distance, chip_select)

    def stats(h, distance):
        chips(h, distance, chip_stats)

    def stats_send(h):
        for k in (4, 3, 5, 2, 6, 1, 7):
            device = (at.along_z(k), at.mp)
            send(st_own.at[h], st_all.at[h, at.dp], sent.at[8 + h], sr.at[h, at.z], device)
        send(st_own.at[h], st_all.at[h, at.dp], sent.at[10 + h], scr.at[h], here)

    def stats_forward(h):
        for k in (1, 7, 2, 6, 3, 5, 4):
            origin = at.along_z(k)
            landed(st_all.at[h, origin], sr.at[h, wrap(at.z + k, ZN)])
            send(st_all.at[h, origin], st_all.at[h, origin], sent.at[10 + h], scr.at[h], here)

    def stats_arrived(h):
        landed(st_all.at[h, pl.ds(0, ZN)], scr.at[h])
        st_all[h, at.dp] = st_own[h]

    def merged(h, i):
        code = tab[2, pl.ds(i, 1), :]
        partner = jnp.bitwise_and(jnp.right_shift(code, 5), 31)
        owner = jnp.right_shift(partner, 1)
        turned = pltpu.roll(owner, SPAN, 1)
        straight = jnp.zeros((2, PAIR), F32)
        crossed = jnp.zeros((2, PAIR), F32)
        for o in range(DP):
            pair = st_all[h, o, pl.ds(i * 2, 2), :]
            straight = jnp.where(owner == o, pair, straight)
            crossed = jnp.where(turned == o, pair, crossed)
        same = (jnp.bitwise_and(partner, 1) == 0) == low
        there = jnp.where(same, straight, pltpu.roll(crossed, SPAN, 1))
        own = st_own[h, pl.ds(i * 2, 2), :]
        lse_here, lse_there = own[:1], there[:1]
        top = jnp.maximum(lse_here, lse_there)
        lse = top + jnp.log(jnp.exp(lse_here - top) + jnp.exp(lse_there - top))
        delta = jnp.exp(lse_here - lse) * own[1:] + jnp.exp(lse_there - lse) * there[1:]
        return lse, delta

    def chip_grads(h, chip):
        codes = lane_codes(chip)
        block = jnp.where(jnp.right_shift(codes, 10) > 0, blocks_of(codes), NB_DEV)
        parts = [merged(h, chip * 2 + core) for core in (0, 1)]
        lse = jnp.concatenate([p[0] for p in parts], axis=1)
        delta = jnp.concatenate([p[1] for p in parts], axis=1)
        prob = jnp.exp(score_sv[h, chip] - lse)
        score_grad = prob * (pgrad_sv[h, chip] - delta) * SCALE
        zero = jnp.zeros_like(prob)
        prob_by_block = jnp.concatenate(
            [jnp.where(block == b, prob, zero).astype(BF16) for b in range(NB_DEV)], axis=0
        )
        grad_by_block = jnp.concatenate(
            [jnp.where(block == b, score_grad, zero).astype(BF16) for b in range(NB_DEV)], axis=0
        )
        acc[:, :HD] += dot(grad_by_block, q_sel[h, chip], NN)
        acc[:, HD:] += dot(prob_by_block, g_sel[h, chip], NN)
        dq = jnp.transpose(dot(kt[h], grad_by_block, NN)).astype(BF16)
        for core in (0, 1):
            dqs[h, chip * 2 + core] = dq[core * PAIR : (core + 1) * PAIR, :]

    def grads_begin(h):
        acc[...] = jnp.zeros_like(acc)

    def grads_part(h, begin, end, sends):
        def one(t, carry):
            chip = lax.rem(at.z + 1 + t, ZN)
            chip_grads(h, chip)
            if sends:
                for core in (0, 1):
                    dq_copy(h, chip * 2 + core)
            return carry

        lax.fori_loop(begin, end, one, 0)

    def grads_end(h):
        chip_grads(h, at.z)
        dqr[h, at.dp] = dqs[h, at.dp]
        bg[h] = acc[...].astype(BF16)

    def dq_copy(h, i):
        send(dqs.at[h, i], dqr.at[h, at.dp], sent.at[12 + h], dqrs.at[h], (i, at.mp))

    def dq_send(h, offsets):
        for offset in offsets:
            for other_core in (False, True):
                if offset == 0 and not other_core:
                    continue
                i = at.along_z(offset, other_core)
                dq_copy(h, i)

    def dq_final(h):
        landed(dqr.at[h, pl.ds(0, DP - 1)], dqrs.at[h])

        def one(c, carry):
            places = [tab[3, pl.ds(c * K + k, 1), :] for k in range(K)]
            total = jnp.zeros((SPAN, HD), BF16)
            for m in range(2 * DP):
                hit = (places[0] == m) | (places[1] == m)
                factor = jnp.where(hit, 1.0, 0.0).astype(BF16)
                total = total + dqr[h, m // 2, pl.ds(m % 2 * SPAN, SPAN), :] * factor
            dq_out[pl.ds(pl.multiple_of(c * SPAN, SPAN), SPAN), own_cols[h]] = total
            return carry

        lax.fori_loop(0, ROWS // SPAN, one, 0)

    def weight_sibling(h, begin, end):
        def one(which, carry):
            near = lax.div(which + 1, 2)
            sign = 2 * lax.rem(which, 2) - 1
            target = wrap(at.z + sign * (4 - near), ZN)
            csb[h, target] = dot(enc[target * 2 + 1 - at.core], bg[h], TN).astype(BF16)
            send(csb.at[h, target], crb.at[h, target], sent.at[14 + h], wcr.at[h, near], here)
            return carry

        lax.fori_loop(begin, end, one, 0)

    def weight_met(h, near):
        landed(crb.at[h, pl.ds(0, 1 if near in (0, 4) else 2)], wcr.at[h, near])

    def weight_term(h, which):
        target = wrap(at.z + RING[which], ZN)
        return dot(enc[target * 2 + at.core], bg[h], TN) + crb[h, target].astype(F32)

    def z_region(step, way):
        return pl.ds(way * CHUNK, CHUNK) if step == 1 else pl.ds(0, SHARD)

    def weight_put(h, way, step, value):
        region = z_region(step, way)
        zsb[h, way, step - 1, region, :] = value.astype(BF16)
        send(
            zsb.at[h, way, step - 1, region], zrb.at[h, way, step - 1, region],
            sent.at[16 + h], wzr.at[h, way, step - 1], at.z_device(way),
        )

    def weight_step(h, step):
        if step == 1:
            weight_met(h, 0)
            value = weight_term(h, 0)
            for way in (0, 1):
                weight_put(h, way, 1, value[way * CHUNK : (way + 1) * CHUNK, :])
            return
        weight_met(h, step - 1)
        for way in (0, 1):
            which = 2 * step - 3 + way
            value = weight_term(h, which)
            region = z_region(step - 1, way)
            landed(zrb.at[h, way, step - 2, region], wzr.at[h, way, step - 2])
            came = zrb[h, way, step - 2, region, :].astype(F32)
            if step == 2:
                pieces = [value[:CHUNK, :], value[CHUNK:, :]]
                pieces[way] = pieces[way] + came
                value = jnp.concatenate(pieces, axis=0)
            else:
                value = value + came
            weight_put(h, way, step, value)

    def weight_final(h):
        weight_met(h, 4)
        value = weight_term(h, 7)
        for way in (0, 1):
            landed(zrb.at[h, way, 3], wzr.at[h, way, 3])
            value = value + zrb[h, way, 3].astype(F32)
        kg_out[:, own_cols[h]] = value[:, :HD]
        vg_out[:, own_cols[h]] = value[:, HD:]

    def width_part(path, offset, j):
        if path == 0:
            index = wrap(at.x + offset, SIDE) * SIDE + j
        else:
            index = j * SIDE + wrap(at.y + offset, SIDE)
        cols = pl.ds(pl.multiple_of(index * SHARD, SHARD), SHARD)
        return sum(dot(bg[h, rows_of(path), :], w[h, cols, :], NT) for h in range(HEADS))

    def width_far(path):
        def one(j, carry):
            value = width_part(path, 2, j).astype(BF16)
            for way in (0, 1):
                xs1[path, way, j] = value[way * CHUNK : (way + 1) * CHUNK, :]
            return carry

        lax.fori_loop(0, SIDE, one, 0)
        for way in (0, 1):
            device = (at.dp, at.plane_neighbour(path, 0, way))
            send(xs1.at[path, way], xr1.at[path, way], sent.at[18], x1r.at[path, way], device)

    def width_near(path):
        for way in (0, 1):
            def one(j, carry):
                value = width_part(path, 1 if way == 0 else -1, j)
                pieces = [value[:CHUNK, :], value[CHUNK:, :]]
                xs2[path, way, 1 - way, j] = pieces[1 - way].astype(BF16)
                near[path, way, j] = pieces[way]
                return carry

            lax.fori_loop(0, SIDE, one, 0)
            near_send(path, way, 1 - way)

    def near_send(path, way, part):
        device = (at.dp, at.plane_neighbour(path, 0, way))
        send(xs2.at[path, way, part], xr2.at[path, way, part], sent.at[19], x2r.at[path], device)

    def width_met(path, way):
        landed(xr1.at[path, way], x1r.at[path, way])
        for j in range(SIDE):
            xs2[path, way, way, j] = (near[path, way, j] + xr1[path, way, j].astype(F32)).astype(BF16)
        near_send(path, way, way)

    def second(path):
        return at.y if path == 0 else at.x

    def width_own(path):
        def one(j, carry):
            group[path, j] = width_part(path, 0, j)
            return carry

        lax.fori_loop(0, SIDE, one, 0)

    def second_send(path, way, part):
        device = (at.dp, at.plane_neighbour(path, 1, way))
        send(ys2.at[path, way, part], yr2.at[path, way, part], sent.at[21], y2r.at[path], device)

    def second_near(path, way):
        return wrap(second(path) + (1 if way == 0 else -1), SIDE)

    def width_turn(path):
        landed(xr2.at[path], x2r.at[path])

        def one(j, carry):
            for part in (0, 1):
                rows = pl.ds(part * CHUNK, CHUNK)
                came = xr2[path, 0, part, j].astype(F32) + xr2[path, 1, part, j].astype(F32)
                group[path, j, rows, :] += came
            return carry

        lax.fori_loop(0, SIDE, one, 0)
        far = wrap(second(path) + 2, SIDE)
        for way in (0, 1):
            ys1[path, way] = group[path, far, pl.ds(way * CHUNK, CHUNK), :].astype(BF16)
            device = (at.dp, at.plane_neighbour(path, 1, way))
            send(ys1.at[path, way], yr1.at[path, way], sent.at[20], y1r.at[path, way], device)
        for way in (0, 1):
            part = 1 - way
            piece = group[path, second_near(path, way), pl.ds(part * CHUNK, CHUNK), :]
            ys2[path, way, part] = piece.astype(BF16)
            second_send(path, way, part)

    def width_second(path):
        for way in (0, 1):
            landed(yr1.at[path, way], y1r.at[path, way])
            piece = group[path, second_near(path, way), pl.ds(way * CHUNK, CHUNK), :]
            ys2[path, way, way] = (piece + yr1[path, way].astype(F32)).astype(BF16)
            second_send(path, way, way)

    def width_final(path):
        landed(yr2.at[path], y2r.at[path])
        for part in (0, 1):
            value = group[path, second(path), pl.ds(part * CHUNK, CHUNK), :]
            for way in (0, 1):
                value = value + yr2[path, way, part].astype(F32)
            eg_out[pl.ds(path * HALF + part * CHUNK, CHUNK), :] = value.astype(BF16)

    def finish():
        for h in range(HEADS):
            landed(q_all.at[h, pl.ds(0, 14)], sent.at[h])
            landed(q_all.at[h], sent.at[2 + h])
            landed(st_all.at[h, pl.ds(0, ZN - 1)], sent.at[8 + h])
            landed(st_all.at[h, pl.ds(0, ZN)], sent.at[10 + h])
            landed(dqr.at[h, pl.ds(0, DP - 1)], sent.at[12 + h])
            landed(crb.at[h], sent.at[14 + h])
            landed(crb.at[h, pl.ds(0, 7)], sent.at[16 + h])
        landed(ids_all.at[pl.ds(0, 7)], sent.at[4])
        landed(ids_all.at[pl.ds(0, ZN)], sent.at[5])
        landed(enc.at[pl.ds(0, 3)], sent.at[6])
        landed(enc.at[pl.ds(0, 12)], sent.at[7])
        for n, ref in enumerate((xr1, xr2, yr1, yr2)):
            landed(ref, sent.at[18 + n])

    for way in (0, 1):
        ids_send(way, 1)
    z_start(0)
    ids_core(at.dp)
    for path in (0, 1):
        p1_first(path)
    for path in (0, 1):
        p2_first(path, 0)
    pltpu.make_async_copy(e_ref, enc.at[at.mp], local_sem.at[0]).start()
    for h in range(HEADS):
        cols = own_cols[h]
        pltpu.make_async_copy(q_ref.at[:, cols], q_all.at[h, at.dp], local_sem.at[1]).start()
        pltpu.make_async_copy(g_ref.at[:, cols], g_all.at[h, at.dp], local_sem.at[1]).start()
        pltpu.make_async_copy(kw_ref.at[:, cols], w.at[h, :, pl.ds(0, HD)], local_sem.at[2]).start()
        pltpu.make_async_copy(vw_ref.at[:, cols], w.at[h, :, pl.ds(HD, HD)], local_sem.at[2]).start()

    for way in (0, 1):
        for path in (0, 1):
            p1_arrive(path, way)
    z_arrive(1, 0, 0)
    z_arrive(1, 0, 1)
    z_start(1)
    for path in (0, 1):
        p2_arrive(path, 0)
    ids_arrive(1)
    for path in (0, 1):
        p1_far(path)
    z_arrive(2, 0, 0)
    landed(enc.at[0], local_sem.at[0])
    landed(q_all.at[0, pl.ds(0, 4)], local_sem.at[1])
    landed(w, local_sem.at[2])
    ids_arrive(2)
    z_arrive(2, 0, 1)
    for path in (0, 1):
        p2_arrive(path, 1)
    for path in (0, 1):
        project_near(path, 0)
    ids_arrive(3)
    z_arrive(3, 0, 0)
    for path in (0, 1):
        p2_arrive(path, 2)
    for path in (0, 1):
        project_near(path, 1)
    ids_arrive(4)
    z_arrive(3, 0, 1)
    for path in (0, 1):
        p2_arrive(path, 3)
    for path in (0, 1):
        project_near(path, 2)
    make_tables()
    z_arrive(1, 1, 0)
    select(0, 0)
    z_arrive(1, 1, 1)
    for path in (0, 1):
        project_near(path, 3)
    p2_far()
    project_far()
    stats(0, 0)
    z_arrive(4, 0, 0)
    z_arrive(4, 0, 1)
    z_arrive(2, 1, 0)
    select(0, 1)
    stats(0, 1)
    select(0, 2)
    stats(0, 2)
    stats_send(0)
    z_arrive(2, 1, 1)
    z_arrive(3, 1, 0)
    select(1, 0)
    stats_forward(0)
    z_arrive(3, 1, 1)
    stats(1, 0)
    stats_arrived(0)
    grads_begin(0)
    grads_part(0, 0, 4, True)
    z_arrive(4, 1, 0)
    z_arrive(4, 1, 1)
    grads_part(0, 4, 7, False)
    grads_end(0)
    weight_sibling(0, 0, 3)
    select(1, 1)
    stats(1, 1)
    select(1, 2)
    stats(1, 2)
    stats_send(1)
    weight_step(0, 1)
    dq_send(0, (5, 6))
    weight_sibling(0, 3, 8)
    stats_forward(1)
    dq_send(0, (7, 0))
    weight_step(0, 2)
    stats_arrived(1)
    grads_begin(1)
    grads_part(1, 0, 7, False)
    grads_end(1)
    weight_sibling(1, 0, 3)
    width_far(0)
    width_far(1)
    weight_step(0, 3)
    weight_step(1, 1)
    dq_send(1, (4, 0))
    width_near(0)
    width_near(1)
    weight_step(0, 4)
    dq_send(1, (1, 5))
    weight_sibling(1, 3, 8)
    weight_step(1, 2)
    dq_send(1, (2, 6))
    width_own(0)
    width_own(1)
    for way in (0, 1):
        for path in (0, 1):
            width_met(path, way)
    weight_step(1, 3)
    dq_send(1, (3, 7))
    weight_final(0)
    dq_final(0)
    for path in (0, 1):
        width_turn(path)
    weight_step(1, 4)
    for path in (0, 1):
        width_second(path)
    dq_final(1)
    for path in (0, 1):
        width_final(path)
    weight_final(1)
    finish()


def publish_kernel(a, b, c, d, a_out, b_out, c_out, d_out, a_mid, b_mid, c_mid, d_mid, came, left):
    arrays = ((a, a_mid, a_out), (b, b_mid, b_out), (c, c_mid, c_out), (d, d_mid, d_out))
    loads = [pltpu.make_async_copy(x[0], x[1], came.at[n]) for n, x in enumerate(arrays)]
    stores = [pltpu.make_async_copy(x[1], x[2], left.at[n]) for n, x in enumerate(arrays)]
    for load in loads:
        load.start()
    for load, store in zip(loads, stores):
        load.wait()
        store.start()
    for store in stores:
        store.wait()


def body(queries, grad_attn, encoded, key_weight, value_weight, nbr_ids):
    hbm = pl.BlockSpec(memory_space=pltpu.HBM)
    vmem = pl.BlockSpec(memory_space=pltpu.VMEM)
    dma = pltpu.SemaphoreType.DMA
    shapes = (
        jax.ShapeDtypeStruct((ROWS, SHARD), BF16),
        jax.ShapeDtypeStruct((ROWS, SHARD), BF16),
        jax.ShapeDtypeStruct((SHARD, SHARD), F32),
        jax.ShapeDtypeStruct((SHARD, SHARD), F32),
    )
    ids = jnp.pad(nbr_ids.reshape(1, DP), ((0, 7), (0, 128 - DP)))
    results = pl.pallas_call(
        kernel,
        out_shape=shapes,
        in_specs=[vmem] + [hbm] * 5,
        out_specs=(vmem, vmem, vmem, vmem),
        scratch_shapes=[
            pltpu.VMEM((HEADS, DP, ROWS, HD), BF16),
            pltpu.VMEM((HEADS, DP, ROWS, HD), BF16),
            pltpu.VMEM((DP, 8, 128), I32),
            pltpu.VMEM((4, DP, 128), I32),
            pltpu.VMEM((MP, ROWS, SHARD), BF16),
            pltpu.VMEM((HEADS, MP * SHARD, 2 * HD), BF16),
            pltpu.VMEM((HEADS, ROWS, 2 * HD), F32),
            pltpu.VMEM((ROWS, 2 * HD), F32),
            pltpu.VMEM((HEADS, ROWS, 2 * HD), BF16),
            pltpu.VMEM((HEADS, HD, ROWS), BF16),
            pltpu.VMEM((HEADS, ZN, 2 * PAIR, HD), BF16),
            pltpu.VMEM((HEADS, ZN, 2 * PAIR, HD), BF16),
            pltpu.VMEM((HEADS, ZN, NL, 2 * PAIR), F32),
            pltpu.VMEM((HEADS, ZN, NL, 2 * PAIR), F32),
            pltpu.VMEM((HEADS, DP * 2, PAIR), F32),
            pltpu.VMEM((HEADS, DP, DP * 2, PAIR), F32),
            pltpu.VMEM((HEADS, DP, PAIR, HD), BF16),
            pltpu.VMEM((HEADS, DP, PAIR, HD), BF16),
            pltpu.VMEM((HEADS, ROWS, 2 * HD), BF16),
            pltpu.VMEM((HEADS, ZN, SHARD, 2 * HD), BF16),
            pltpu.VMEM((HEADS, ZN, SHARD, 2 * HD), BF16),
            pltpu.VMEM((HEADS, 2, 4, SHARD, 2 * HD), BF16),
            pltpu.VMEM((HEADS, 2, 4, SHARD, 2 * HD), BF16),
            pltpu.VMEM((2, 2, SIDE, CHUNK, SHARD), BF16),
            pltpu.VMEM((2, 2, SIDE, CHUNK, SHARD), BF16),
            pltpu.VMEM((2, 2, SIDE, CHUNK, SHARD), F32),
            pltpu.VMEM((2, 2, 2, SIDE, CHUNK, SHARD), BF16),
            pltpu.VMEM((2, 2, 2, SIDE, CHUNK, SHARD), BF16),
            pltpu.VMEM((2, SIDE, HALF, SHARD), F32),
            pltpu.VMEM((2, 2, CHUNK, SHARD), BF16),
            pltpu.VMEM((2, 2, CHUNK, SHARD), BF16),
            pltpu.VMEM((2, 2, 2, CHUNK, SHARD), BF16),
            pltpu.VMEM((2, 2, 2, CHUNK, SHARD), BF16),
            dma((3,)), dma((22,)),
            dma((HEADS, 2, 2, 4)), dma((HEADS, 3)),
            dma((2, 4)), dma((1,)),
            dma((2, 2)), dma((2,)), dma((2, 4, 2)), dma((1,)),
            dma((HEADS, ZN)), dma((HEADS,)), dma((HEADS,)),
            dma((HEADS, 5)), dma((HEADS, 2, 4)),
            dma((2, 2)), dma((2,)), dma((2, 2)), dma((2,)),
        ],
        compiler_params=pltpu.CompilerParams(
            collective_id=0, has_side_effects=True, vmem_limit_bytes=60 * 2**20
        ),
        name="retro_backward",
    )(ids, queries, grad_attn, encoded, key_weight, value_weight)
    return pl.pallas_call(
        publish_kernel,
        out_shape=shapes,
        in_specs=[hbm] * 4,
        out_specs=(hbm,) * 4,
        scratch_shapes=[pltpu.VMEM(x.shape, x.dtype) for x in shapes] + [dma((4,)), dma((4,))],
        name="publish",
    )(*results)


def solution(mesh):
    return jax.shard_map(
        body,
        mesh=mesh,
        in_specs=(
            P("dp", "mp"),
            P("dp", "mp"),
            P("dp", "mp"),
            P(None, "mp"),
            P(None, "mp"),
            P("dp", None),
        ),
        out_specs=(P("dp", "mp"), P("dp", "mp"), P("dp", "mp"), P("dp", "mp")),
        check_vma=False,
    )
```
